128 devices in a mesh: section: 8 (over x, core), dp: 16 (over z, y).
Axes of the slice: x: 4, y: 4, z: 4, core: 2. Of those that a mesh axis runs over, the one named last changes fastest.
Arguments:
- layer_inputs: bfloat16 [8, 4, 64, 6144], P('section', None, None, 'dp'), may hold values from -6 to 6
- expert_ids: int32 [8, 4, 64, 2], P('section'), may hold values from 0 to 7, as said below
- hidden: bfloat16 [8, 4, 32, 8192], P('section', None, None, 'dp'), may hold values from -6 to 6
- down_weight: bfloat16 [8, 6144, 8192], P('section', None, 'dp'), may hold values from -0.0625 to 0.0625
- router_weight: bfloat16 [8, 6144, 8], P('section', 'dp'), may hold values from -0.078125 to 0.078125
- grad_out: bfloat16 [4, 64, 6144], P(None, None, 'dp'), may hold values from -1.796875 to 1.796875
Outputs:
- input_grad: bfloat16 [4, 64, 6144], P(None, 'section', 'dp')
- hidden_grad: bfloat16 [8, 4, 32, 8192], P('section', None, None, 'dp')
- down_grad: bfloat16 [8, 6144, 8192], P('section', None, 'dp')
- router_grad: float32 [8, 6144, 8], P('section', 'dp')
The draws below stay inside these ranges and needn't reach their ends.
Inputs may be any that keep to these rules, and one draw needn't show every extreme that they name: `expert_ids`: the 2 ids of a token differ. In each layer and micro-batch expert 0 is named by 16 to 32 tokens, and in at least one micro-batch of every layer by exactly 32.
All inputs are finite; a program needn't handle non-finite values.
Results may differ from the reference program's by a relative error of at most 0.0062.
Values may be sent and summed in bfloat16 or wider, within the bound.
No kernel may reach another device: no remote copies, remote signals or barrier semaphores. Data moves between devices by JAX's collectives and lax.ppermute only.
A program may use at most 64 MiB of HBM per device.

```python
import jax
import jax.numpy as jnp

D = 6144
EXPERTS = 8
FFW = 8192
MICRO = 4
TOK_MB = 64
CAP = 32
LAYERS = 8


def draw_expert_ids(key, part):
    key = jax.random.fold_in(key, 11)
    keys = jax.random.split(key, 6)
    counts = jax.random.randint(keys[0], (LAYERS, MICRO), CAP // 2, CAP + 1)
    full_at = jax.random.randint(keys[1], (LAYERS, 1), 0, MICRO)
    counts = jnp.where(jnp.arange(MICRO, dtype=jnp.int32)[None, :] == full_at, CAP, counts)
    noise = jax.random.randint(keys[2], (LAYERS, MICRO, TOK_MB), 0, TOK_MB)
    distinct = noise * TOK_MB + jnp.arange(TOK_MB, dtype=jnp.int32)[None, None, :]
    order = jnp.argsort(distinct, axis=-1, stable=True)
    rank = jnp.argsort(order, axis=-1, stable=True)
    member = rank < counts[..., None]
    first = jax.random.randint(keys[3], (LAYERS, MICRO, TOK_MB), 1, EXPERTS)
    step = jax.random.randint(keys[4], (LAYERS, MICRO, TOK_MB), 1, EXPERTS - 1)
    second = 1 + (first - 1 + step) % (EXPERTS - 1)
    flip = jax.random.randint(keys[5], (LAYERS, MICRO, TOK_MB), 0, 2)
    low = jnp.where(member, 0, first)
    high = jnp.where(member, first, second)
    left = jnp.where(flip == 1, high, low)
    right = jnp.where(flip == 1, low, high)
    return jnp.stack([left, right], axis=-1).astype(jnp.int32)


def block_scale(own_key, dims, cuts, least, high):
    level, own = 1.0, jax.random.fold_in(own_key, 6)
    for axis_at, parts in cuts:
        steps = jnp.exp(jax.random.uniform(jax.random.fold_in(own, axis_at), (parts,), jnp.float32, least / len(cuts), high / len(cuts)))
        level = level * jnp.repeat(steps, dims[axis_at] // parts).reshape([-1 if axis == axis_at else 1 for axis in range(len(dims))])
    return level


def normal_values(rng, shape, deviation, bound, pieces=(), kind=jnp.bfloat16):
    drawn = deviation * jax.random.normal(rng, shape, jnp.float32)
    if pieces:
        drawn = drawn * block_scale(rng, shape, pieces, -0.22, 0.18)
    return jnp.clip(drawn, -bound, bound).astype(kind)


def setup_inputs(seed: int = 0) -> dict:
    key_list = jax.random.split(jax.random.key(seed), 7)
    return {
        "layer_inputs": normal_values(key_list[0], (LAYERS, MICRO, TOK_MB, D), 1.0, 6.0, ((0, 8), (3, 16))),
        "expert_ids": draw_expert_ids(jax.random.fold_in(key_list[6], 71), 0),
        "hidden": normal_values(key_list[2], (LAYERS, MICRO, CAP, FFW), 1.0, 6.0, ((0, 8), (3, 16))),
        "down_weight": normal_values(key_list[3], (LAYERS, D, FFW), FFW ** -0.5, 0.0625, ((0, 8), (2, 16))),
        "router_weight": normal_values(key_list[4], (LAYERS, D, EXPERTS), D ** -0.5, 0.078125, ((0, 8), (1, 16))),
        "grad_out": normal_values(key_list[5], (MICRO, TOK_MB, D), 0.3, 1.796875, ((2, 16),)),
    }


def layer_back(x_rows, routes, stored, upstream, weights, router):
    member = ((routes[..., 0] == 0) | (routes[..., 1] == 0)).astype(jnp.int32)
    position = (jnp.cumsum(member, axis=1) - member).astype(jnp.int32)
    slot_range = jnp.arange(CAP, dtype=jnp.int32)
    picks = ((position[:, None, :] == slot_range[None, :, None]) & (member[:, None, :] > 0)).astype(jnp.float32)
    logits = jnp.einsum('mtd,de->mte', x_rows.astype(jnp.float32), router.astype(jnp.float32))
    expert_range = jnp.arange(EXPERTS, dtype=jnp.int32)
    other = jnp.where(routes[..., 0] == 0, routes[..., 1], routes[..., 0])
    other_hot = (other[..., None] == expert_range).astype(jnp.float32)
    own_hot = (expert_range == 0).astype(jnp.float32)
    gate = 1.0 / (1.0 + jnp.exp(jnp.sum(other_hot * logits, axis=-1) - logits[..., 0]))
    gate_slot = jnp.einsum('mct,mt->mc', picks, gate)
    rows = jnp.einsum('mct,mtd->mcd', picks, upstream.astype(jnp.float32)).astype(jnp.bfloat16)
    product = jnp.einsum('mcd,df->mcf', rows.astype(jnp.float32), weights.astype(jnp.float32))
    score = jnp.sum(stored.astype(jnp.float32) * product, axis=-1)
    hidden_part = (gate_slot[..., None] * product).astype(jnp.bfloat16)
    weighted = (gate_slot[..., None] * rows.astype(jnp.float32)).astype(jnp.bfloat16)
    down_part = jnp.einsum('mcd,mcf->df', weighted.astype(jnp.float32), stored.astype(jnp.float32)).astype(jnp.bfloat16)
    token_score = jnp.einsum('mct,mc->mt', picks, score)
    delta = gate * (1.0 - gate) * token_score
    logit_grads = (delta[..., None] * (own_hot - other_hot)).astype(jnp.bfloat16)
    router_part = jnp.einsum('mtd,mte->de', x_rows.astype(jnp.float32), logit_grads.astype(jnp.float32))
    passed = (upstream.astype(jnp.float32) + jnp.einsum('mte,de->mtd', logit_grads.astype(jnp.float32), router.astype(jnp.float32))).astype(jnp.bfloat16)
    return passed, hidden_part, down_part, router_part


def reference(layer_inputs, expert_ids, hidden, down_weight, router_weight, grad_out):
    upstream = grad_out
    hidden_grads = []
    down_grads = []
    router_grads = []
    for layer_index in range(LAYERS - 1, -1, -1):
        passed, hidden_part, down_part, router_part = layer_back(layer_inputs[layer_index], expert_ids[layer_index], hidden[layer_index], upstream, down_weight[layer_index], router_weight[layer_index])
        hidden_grads.append(hidden_part)
        down_grads.append(down_part)
        router_grads.append(router_part)
        upstream = passed
    hidden_grad = jnp.stack(hidden_grads[::-1], axis=0)
    down_grad = jnp.stack(down_grads[::-1], axis=0)
    router_grad = jnp.stack(router_grads[::-1], axis=0)
    return upstream, hidden_grad, down_grad, router_grad
```

```python
import jax
import jax.numpy as jnp
from jax import lax
from jax.sharding import PartitionSpec as P

F32 = jnp.float32
BF16 = jnp.bfloat16


def nt(a, b):
    return lax.dot_general(a, b, (((1,), (1,)), ((), ())), preferred_element_type=F32)


def tn(a, b):
    return lax.dot_general(a, b, (((0,), (0,)), ((), ())), preferred_element_type=F32)


def nn(a, b):
    return jnp.dot(a, b, preferred_element_type=F32)


def to_all(value, axes, count):
    copies = jnp.broadcast_to(value[None], (count,) + value.shape)
    return lax.all_to_all(copies, axes, 0, 0, tiled=True)


def pieces(value):
    first = lax.reduce_precision(value, 8, 7)
    rest = value - first
    second = lax.reduce_precision(rest, 8, 7)
    return [first.astype(BF16), second.astype(BF16), (rest - second).astype(BF16)]


def slot_picks(codes, micro, tok, cap):
    tokens = micro * tok
    row = lax.broadcasted_iota(jnp.int32, (tokens, tokens), 0)
    col = lax.broadcasted_iota(jnp.int32, (tokens, tokens), 1)
    before = ((row < col) & (row // tok == col // tok)).astype(BF16)
    member = codes > 0.0
    rank = nn(member.astype(BF16), before).astype(jnp.int32)
    base = (lax.broadcasted_iota(jnp.int32, (1, tokens), 1) // tok) * cap
    slot = jnp.where(member, rank + base, -1)
    slots = lax.broadcasted_iota(jnp.int32, (1, micro * cap, 1), 1)
    return (slot[:, None, :] == slots).astype(BF16)


def per_device(layer_inputs, expert_ids, hidden, down_weight, router_weight, grad_out):
    sections, ways = lax.axis_size("section"), lax.axis_size("dp")
    me = lax.axis_index("section")
    micro, tok, width = grad_out.shape
    cap, units = hidden.shape[2:]
    experts = router_weight.shape[2]
    tokens, slots = micro * tok, micro * cap
    x = layer_inputs[0].reshape(tokens, width)
    ids = expert_ids[0].reshape(tokens, 2)
    hid = hidden[0].reshape(slots, units)
    weights = down_weight[0].reshape(ways, width, units)
    router = router_weight[0].T
    grads = grad_out.reshape(tokens, width)

    other = jnp.where(ids[:, 0] == 0, ids[:, 1], ids[:, 0])
    member = (ids[:, 0] == 0) | (ids[:, 1] == 0)
    code = jnp.where(member, other, 0).astype(F32)
    code_row = jnp.pad(code.astype(BF16), (0, width - tokens))[None]
    got = to_all(jnp.concatenate([router, code_row]), "section", sections)
    routers = got[:, :experts]
    codes = got[:, experts, :tokens].astype(F32)
    picks = slot_picks(codes, micro, tok, cap)
    pick = slot_picks(code[None], micro, tok, cap)[0]

    expert_col = jnp.arange(experts, dtype=F32)[:, None]
    sign_own = (expert_col == 0).astype(F32) - (expert_col == code[None]).astype(F32)
    apart = -jnp.sum(sign_own * nt(router, x), axis=0)
    parts = jnp.stack(pieces(apart))
    parts = jnp.pad(nt(parts, pick).astype(BF16), ((0, experts - 3), (0, width - slots)))
    rows = nn(pick, grads).astype(BF16)
    block = jnp.concatenate([rows, routers[1:].reshape(-1, width), parts])
    got = to_all(block, "dp", ways)

    both = jnp.einsum("pkd,pdf->kf", got, weights, preferred_element_type=F32)
    product, mixed = both[:slots], both[slots:-experts]
    apart = jnp.sum(got[:, -experts:, :slots].astype(F32), axis=(0, 1))
    filled = jnp.sum(pick.astype(F32), axis=1)
    gate = filled / (1.0 + jnp.exp(apart))
    base = jnp.sum(hid.astype(F32) * product, axis=1)
    cross = nt(mixed.astype(BF16), hid).reshape(sections - 1, experts, slots)
    code_slot = nt(codes.astype(BF16), pick)
    signs = (expert_col == 0).astype(F32)[None] - (
        expert_col[None] == code_slot[:, None, :]
    ).astype(F32)
    above = jnp.arange(sections) > me
    signs = jnp.where(above[:, None, None], signs, 0.0)[1:]
    coefs = jnp.sum(signs * cross, axis=1)
    table = jnp.concatenate([base[None], coefs]) * (gate * (1.0 - gate))[None]
    got_table = to_all(table, ("section", "dp"), sections * ways)
    table = jnp.sum(got_table.reshape(sections, ways, sections, slots), axis=1)

    table = jnp.einsum(
        "skc,sct->skt", table, picks.astype(F32), precision=lax.Precision.HIGHEST
    )
    deltas = [None] * sections
    for layer in range(sections - 1, -1, -1):
        value = table[layer, 0]
        for upper in range(layer + 1, sections):
            value = value + deltas[upper] * table[layer, upper]
        deltas[layer] = lax.reduce_precision(value, 8, 7)
    deltas = jnp.stack(deltas)

    delta_slot = nt(deltas.astype(BF16), pick)
    lift = (signs * delta_slot[1:, None, :]).reshape(-1, slots).astype(BF16)
    scaled = (gate[:, None] * hid.astype(F32)).astype(BF16)
    right = jnp.concatenate([scaled, nn(lift, scaled).astype(BF16)])
    down_grad = jnp.einsum(
        "pkd,kf->pdf", got[:, :-experts], right, preferred_element_type=F32
    ).astype(BF16)
    hidden_grad = (gate[:, None] * (product + tn(lift, mixed.astype(BF16)))).astype(BF16)

    delta_own = lax.dynamic_index_in_dim(deltas, me, 0, keepdims=True)
    router_grad = nt(x.T, (sign_own * delta_own).astype(BF16))
    mine = tok // sections
    tokens_own = lambda a: lax.dynamic_slice_in_dim(
        a.reshape(a.shape[:-1] + (micro, tok)), me * mine, mine, axis=a.ndim
    )
    code_mine = tokens_own(codes).reshape(sections, 1, micro * mine)
    sign_mine = (expert_col == 0).astype(F32)[None] - (expert_col[None] == code_mine).astype(F32)
    logit_grads = sign_mine * tokens_own(deltas).reshape(sections, 1, micro * mine)
    step = tn(
        logit_grads.reshape(sections * experts, -1).astype(BF16),
        routers.reshape(sections * experts, width),
    )
    grads_mine = lax.dynamic_slice_in_dim(grad_out, me * mine, mine, axis=1)
    input_grad = (grads_mine.astype(F32) + step.reshape(micro, mine, width)).astype(BF16)
    return (
        input_grad,
        hidden_grad.reshape(1, micro, cap, units),
        down_grad.reshape(1, ways * width, units),
        router_grad[None],
    )


def solution(mesh):
    return jax.shard_map(
        per_device,
        mesh=mesh,
        in_specs=(
            P("section", None, None, "dp"),
            P("section", None, None, None),
            P("section", None, None, "dp"),
            P("section", None, "dp"),
            P("section", "dp", None),
            P(None, None, "dp"),
        ),
        out_specs=(
            P(None, "section", "dp"),
            P("section", None, None, "dp"),
            P("section", None, "dp"),
            P("section", "dp", None),
        ),
        check_vma=False,
    )
```

```python
import jax
import jax.numpy as jnp
from jax import lax
from jax.experimental import pallas as pl
from jax.experimental.pallas import tpu as pltpu
from jax.sharding import PartitionSpec as P

F32 = jnp.float32
BF16 = jnp.bfloat16
VMEM = pl.BlockSpec(memory_space=pltpu.VMEM)
SMEM = pl.BlockSpec(memory_space=pltpu.SMEM)
ANY = pl.BlockSpec(memory_space=pl.ANY)
CHUNKS = 8


def nt(a, b):
    return lax.dot_general(a, b, (((1,), (1,)), ((), ())), preferred_element_type=F32)


def tn(a, b):
    return lax.dot_general(a, b, (((0,), (0,)), ((), ())), preferred_element_type=F32)


def nn(a, b):
    return jnp.dot(a, b, preferred_element_type=F32)


def to_all(value, axes, count):
    copies = jnp.broadcast_to(value[None], (count,) + value.shape)
    return lax.all_to_all(copies, axes, 0, 0, tiled=True)


def swaps(value, axis, distances):
    count = lax.axis_size(axis)
    return [value] + [
        lax.ppermute(value, axis, [(i, i ^ d) for i in range(count)]) for d in distances
    ]


def pieces(value):
    first = lax.reduce_precision(value, 8, 7)
    rest = value - first
    second = lax.reduce_precision(rest, 8, 7)
    return [first.astype(BF16), second.astype(BF16), (rest - second).astype(BF16)]


def iota(shape, dim):
    return lax.broadcasted_iota(jnp.int32, shape, dim)


def slot_of(codes, tok, cap):
    tokens = codes.shape[1]
    row, col = iota((tokens, tokens), 0), iota((tokens, tokens), 1)
    before = ((row < col) & (row // tok == col // tok)).astype(F32).astype(BF16)
    member = codes > 0.0
    rank = nn(member.astype(F32).astype(BF16), before).astype(jnp.int32)
    return jnp.where(member, rank + (iota(codes.shape, 1) // tok) * cap, -1)


def expert_signs(codes):
    experts = iota((codes.shape[0], 8, codes.shape[1]), 1).astype(F32)
    return (experts == 0.0).astype(F32) - (experts == codes[:, None, :]).astype(F32)


def diagonal(size):
    return (iota((size, size), 0) == iota((size, size), 1)).astype(F32)


def mid_kernel(me_ref, got_ref, rt_ref, hid_ref, codes_ref, pick_ref, w_ref,
               table_ref, product_ref, mixed_ref, signs_ref, gate_ref, wbuf, sems):
    ways, slots = got_ref.shape[0], hid_ref.shape[0]
    per = ways // CHUNKS
    depth = per * got_ref.shape[2]
    copies = [
        pltpu.make_async_copy(w_ref.at[pl.ds(q * depth, depth)], wbuf.at[q], sems.at[q])
        for q in range(CHUNKS)
    ]
    for copy in copies:
        copy.start()
    me = me_ref[0]
    pick = pick_ref[...]
    code_slot = nt(codes_ref[...].astype(BF16), pick)
    layers = code_slot.shape[0]
    signs = expert_signs(code_slot)
    above = (iota(signs.shape, 0) ^ me) > me
    signs = jnp.where(above, signs, 0.0)
    signs_ref[...] = signs
    filled = nt(jnp.ones((8, pick.shape[1]), BF16), pick)
    apart = jnp.zeros((8, slots), F32)
    for p in range(ways):
        apart += got_ref[p, slots:slots + 8, :slots].astype(F32)
    gate = filled / (1.0 + jnp.exp(jnp.sum(apart, axis=0, keepdims=True)))
    gate_ref[...] = gate
    total = jnp.zeros((slots + rt_ref.shape[1], hid_ref.shape[1]), F32)
    for q in range(CHUNKS):
        copies[q].wait()
        ps = range(q * per, (q + 1) * per)
        left = jnp.concatenate([
            jnp.concatenate([got_ref[p, :slots] for p in ps], axis=1),
            jnp.concatenate([rt_ref[p] for p in ps], axis=1),
        ], axis=0)
        total += nn(left, wbuf[q])
    product, mixed = total[:slots], total[slots:].astype(BF16)
    product_ref[...] = product
    mixed_ref[...] = mixed
    hid = hid_ref[...]
    base = jnp.sum(hid.astype(F32) * product, axis=1, keepdims=True)
    base = jnp.sum(diagonal(slots) * base, axis=0, keepdims=True)
    cross = nt(mixed, hid).reshape(signs.shape)
    coefs = jnp.sum(signs * cross, axis=1)
    table = jnp.where(iota((layers, slots), 0) == 0, base, coefs) * (gate * (1.0 - gate))
    table_ref[...] = jnp.broadcast_to(table[None], table_ref.shape)


def side_kernel(me_ref, got_ref, rt_ref, hid_ref, codes_ref, gate_ref,
                left_ref, picks_ref, scaled_ref, *, tok, cap):
    ways, slots = got_ref.shape[0], hid_ref.shape[0]
    width = got_ref.shape[2]
    me = me_ref[0]
    layers = codes_ref.shape[0]
    slot = slot_of(codes_ref[...], tok, cap)
    for j in range(layers):
        pick = (iota((slots, slot.shape[1]), 0) == slot[j:j + 1]).astype(F32).astype(BF16)
        picks_ref[me ^ j] = pick
    gate_col = jnp.sum(diagonal(slots) * gate_ref[0:1], axis=1, keepdims=True)
    scaled_ref[...] = (gate_col * hid_ref[...].astype(F32)).astype(BF16)
    for p in range(ways):
        left_ref[pl.ds(p * width, width), :] = jnp.concatenate(
            [got_ref[p, :slots], rt_ref[p]], axis=0
        ).T


def tail_kernel(me_ref, got_ref, picks_ref, codes_ref, pick_ref, signs_ref, gate_ref,
                product_ref, mixed_ref, scaled_ref, left_ref, x_ref, here_ref, grads_ref,
                input_ref, hidden_ref, down_ref, router_ref,
                delta_ref, step_ref, obuf, sems):
    layers, slots = codes_ref.shape[0], gate_ref.shape[1]
    tokens = codes_ref.shape[1]
    ways = got_ref.shape[0] // layers
    me = me_ref[0]
    rows = []
    for s in range(layers):
        table = got_ref[s * ways]
        for p in range(1, ways):
            table += got_ref[s * ways + p]
        first = table.astype(BF16)
        rest = table - first.astype(F32)
        second = rest.astype(BF16)
        third = (rest - second.astype(F32)).astype(BF16)
        parts = nn(jnp.concatenate([first, second, third], axis=0), picks_ref[s])
        rows.append(parts[:8] + parts[8:16] + parts[16:])
    deltas = [None] * layers
    for layer in range(layers - 1, -1, -1):
        value = rows[layer][0:1]
        for upper in range(layer + 1, layers):
            value += deltas[upper] * rows[layer][layer ^ upper:(layer ^ upper) + 1]
        deltas[layer] = value.astype(BF16).astype(F32)
        delta_ref[layer:layer + 1, :] = deltas[layer]
    mine = jnp.concatenate([delta_ref[pl.ds(me ^ j, 1), :] for j in range(layers)], axis=0)
    delta_slot = nt(mine.astype(BF16), pick_ref[...])
    lift = (signs_ref[...] * delta_slot[:, None, :]).reshape(layers * 8, slots).astype(BF16)
    scaled = scaled_ref[...]
    right = jnp.concatenate([scaled, nn(lift, scaled).astype(BF16)], axis=0)
    depth = obuf.shape[1]
    copies = []
    for q in range(CHUNKS):
        obuf[q] = nn(left_ref[pl.ds(q * depth, depth), :], right).astype(BF16)
        copies.append(
            pltpu.make_async_copy(obuf.at[q], down_ref.at[pl.ds(q * depth, depth)], sems.at[q])
        )
        copies[-1].start()
    gate_col = jnp.sum(diagonal(slots) * gate_ref[0:1], axis=1, keepdims=True)
    hidden_ref[...] = (gate_col * (product_ref[...] + tn(lift, mixed_ref[...]))).astype(BF16)
    logit_grads = expert_signs(codes_ref[...]) * mine[:, None, :]
    router_ref[...] = nn(logit_grads[0].astype(BF16), x_ref[...])
    step_ref[...] = tn(logit_grads.reshape(layers * 8, tokens).astype(BF16), here_ref[...])
    count = grads_ref.shape[0]
    tok = tokens // count
    own = grads_ref.shape[1]
    for m in range(count):
        step = step_ref[pl.ds(pl.multiple_of(m * tok + me * own, 8), own), :]
        input_ref[m] = (grads_ref[m].astype(F32) + step).astype(BF16)
    for copy in copies:
        copy.wait()


def call(kernel, outs, in_specs, scratch, limit, out_specs=None, flops=0, moved=0):
    return pl.pallas_call(
        kernel,
        out_shape=[jax.ShapeDtypeStruct(*o) for o in outs],
        in_specs=in_specs,
        out_specs=out_specs or [VMEM] * len(outs),
        scratch_shapes=scratch,
        compiler_params=pltpu.CompilerParams(vmem_limit_bytes=limit << 20),
        cost_estimate=pl.CostEstimate(flops=flops, bytes_accessed=moved, transcendentals=0),
    )


def per_device(layer_inputs, expert_ids, hidden, down_weight, router_weight, grad_out):
    sections, ways = lax.axis_size("section"), lax.axis_size("dp")
    me, at = lax.axis_index("section"), lax.axis_index("dp")
    micro, tok, width = grad_out.shape
    cap, units = hidden.shape[2:]
    experts = router_weight.shape[2]
    tokens, slots = micro * tok, micro * cap
    full = ways * width
    x = layer_inputs[0].reshape(tokens, width)
    ids = expert_ids[0].reshape(tokens, 2)
    hid = hidden[0].reshape(slots, units)
    router = router_weight[0].T
    grads = grad_out.reshape(tokens, width)

    got_router = to_all(router, "dp", ways)

    other = jnp.where(ids[:, 0] == 0, ids[:, 1], ids[:, 0])
    member = (ids[:, 0] == 0) | (ids[:, 1] == 0)
    code = jnp.where(member, other, 0).astype(F32)
    code_block = jnp.zeros((1, experts, width), BF16).at[0, 0, :tokens].set(code.astype(BF16))
    slot = slot_of(code[None], tok, cap)
    pick = (slot == iota((slots, 1), 0)).astype(BF16)
    apart = -jnp.sum(expert_signs(code[None])[0] * nt(router, x), axis=0)
    parts = jnp.stack(pieces(apart))
    parts = jnp.pad(nt(parts, pick).astype(BF16), ((0, 16 - 3), (0, width - slots)))
    rows = nn(pick, grads).astype(BF16)
    block = jnp.concatenate([rows, parts])

    block, got_router = lax.optimization_barrier((block, got_router))
    got = to_all(block, "dp", ways)
    layer_blocks = swaps(
        jnp.concatenate([got_router, code_block]), "section", range(1, sections)
    )
    routers = jnp.concatenate([b[:ways] for b in layer_blocks], axis=1)
    codes = jnp.stack([b[ways, 0, :tokens] for b in layer_blocks]).astype(F32)
    here = lax.dynamic_index_in_dim(routers, at, 0, keepdims=False)
    own = tok // sections
    grads_mine = lax.dynamic_slice_in_dim(grad_out, me * own, own, axis=1)
    me_arr = me.astype(jnp.int32).reshape(1)

    depth = full // CHUNKS
    table, product, mixed, signs, gate = call(
        mid_kernel,
        [
            ((sections * ways, sections, slots), F32),
            ((slots, units), F32),
            ((sections * experts, units), BF16),
            ((sections, experts, slots), F32),
            ((8, slots), F32),
        ],
        [SMEM] + [VMEM] * 5 + [ANY],
        [pltpu.VMEM((CHUNKS, depth, units), BF16), pltpu.SemaphoreType.DMA((CHUNKS,))],
        24,
        flops=2 * 192 * full * units,
        moved=full * units * 2,
    )(me_arr, got, routers, hid, codes, pick, down_weight[0])

    got_table = lax.all_to_all(table, ("section", "dp"), 0, 0, tiled=True)

    left, picks, scaled = call(
        lambda *refs: side_kernel(*refs, tok=tok, cap=cap),
        [
            ((full, slots + sections * experts), BF16),
            ((sections, slots, tokens), BF16),
            ((slots, units), BF16),
        ],
        [SMEM] + [VMEM] * 5,
        [],
        24,
        flops=10**9,
        moved=4 * full * 192,
    )(me_arr, got, routers, hid, codes, gate)

    input_grad, hidden_grad, down_grad, router_grad = call(
        tail_kernel,
        [
            ((micro, own, width), BF16),
            ((slots, units), BF16),
            ((full, units), BF16),
            ((experts, width), F32),
        ],
        [SMEM] + [VMEM] * 13,
        [
            pltpu.VMEM((sections, tokens), F32),
            pltpu.VMEM((tokens, width), F32),
            pltpu.VMEM((CHUNKS, depth, units), BF16),
            pltpu.SemaphoreType.DMA((CHUNKS,)),
        ],
        24,
        out_specs=[VMEM, VMEM, ANY, VMEM],
        flops=2 * 192 * full * units,
        moved=full * units * 2,
    )(
        me_arr, got_table, picks, codes, pick, signs, gate,
        product, mixed, scaled, left, x, here, grads_mine,
    )
    return (
        input_grad,
        hidden_grad.reshape(1, micro, cap, units),
        down_grad[None],
        router_grad.T[None],
    )


def solution(mesh):
    return jax.shard_map(
        per_device,
        mesh=mesh,
        in_specs=(
            P("section", None, None, "dp"),
            P("section", None, None, None),
            P("section", None, None, "dp"),
            P("section", None, "dp"),
            P("section", "dp", None),
            P(None, None, "dp"),
        ),
        out_specs=(
            P(None, "section", "dp"),
            P("section", None, None, "dp"),
            P("section", None, "dp"),
            P("section", "dp", None),
        ),
        check_vma=False,
    )
```

```python
import jax
import jax.numpy as jnp
from jax import lax
from jax.experimental import pallas as pl
from jax.experimental.pallas import tpu as pltpu
from jax.sharding import PartitionSpec as P

F32 = jnp.float32
BF16 = jnp.bfloat16
VMEM = pl.BlockSpec(memory_space=pltpu.VMEM)
SMEM = pl.BlockSpec(memory_space=pltpu.SMEM)
HBM = pl.BlockSpec(memory_space=pltpu.HBM)
AUTO = pl.BlockSpec()
RING = (0, 1, 3, 2)
SECTION_STEPS = (2, 6, 4)
LAYER_ORDER = [d ^ core for core in (0, 1) for d in (0,) + SECTION_STEPS]


def nt(a, b):
    return lax.dot_general(a, b, (((1,), (1,)), ((), ())), preferred_element_type=F32)


def tn(a, b):
    return lax.dot_general(a, b, (((0,), (0,)), ((), ())), preferred_element_type=F32)


def nn(a, b):
    return jnp.dot(a, b, preferred_element_type=F32)


def to_all(value, axes, count):
    copies = jnp.broadcast_to(value[None], (count,) + value.shape)
    return lax.all_to_all(copies, axes, 0, 0, tiled=True)


def swap(value, axis, distance):
    count = lax.axis_size(axis)
    return lax.ppermute(value, axis, [(i, i ^ distance) for i in range(count)])


def turn(value, stage, step):
    sections, ways = lax.axis_size("section"), lax.axis_size("dp")
    pairs = []
    for s in range(sections):
        distance = RING[step] * (1 if s % 2 == stage else 4)
        pairs += [(s * ways + p, s * ways + (p ^ distance)) for p in range(ways)]
    return lax.ppermute(value, ("section", "dp"), pairs)


def pieces(value):
    first = lax.reduce_precision(value, 8, 7)
    rest = value - first
    second = lax.reduce_precision(rest, 8, 7)
    return [first.astype(BF16), second.astype(BF16), (rest - second).astype(BF16)]


def iota(shape, dim):
    return lax.broadcasted_iota(jnp.int32, shape, dim)


def slot_of(codes, tok, cap):
    tokens = codes.shape[1]
    row, col = iota((tokens, tokens), 0), iota((tokens, tokens), 1)
    before = ((row < col) & (row // tok == col // tok)).astype(F32).astype(BF16)
    member = codes > 0.0
    rank = nn(member.astype(F32).astype(BF16), before).astype(jnp.int32)
    return jnp.where(member, rank + (iota(codes.shape, 1) // tok) * cap, -1)


def expert_signs(codes):
    experts = iota((codes.shape[0], 8, codes.shape[1]), 1).astype(F32)
    return (experts == 0.0).astype(F32) - (experts == codes[:, None, :]).astype(F32)


def diagonal(size):
    return (iota((size, size), 0) == iota((size, size), 1)).astype(F32)


def block_way(at, odd, far, near):
    plain = RING[near] + 4 * RING[far]
    turned = 4 * RING[near] + RING[far]
    return at ^ jnp.where(odd, turned, plain)


def router_rows(left_ref, right_ref, way):
    return jnp.concatenate(
        [ref[k, way] for ref in (left_ref, right_ref) for k in range(4)], axis=0
    )


def mid_kernel(here_ref, a0, a1, a2, a3, near_ref, far_ref, hid_ref, pick_ref, w_ref,
               table_ref, product_ref, mixed_ref, signs_ref, gate_ref, wbuf, sems):
    slots, width = hid_ref.shape[0], a0.shape[2]
    me, at = here_ref[0], here_ref[1]
    ways = [block_way(at, (me & 1) == 1, far, k) for far in range(4) for k in range(4)]
    copies = [
        pltpu.make_async_copy(
            w_ref.at[pl.ds(pl.multiple_of(way * width, width), width)],
            wbuf.at[j // 2, pl.ds((j % 2) * width, width)],
            sems.at[j],
        )
        for j, way in enumerate(ways)
    ]
    for copy in copies:
        copy.start()
    pick = pick_ref[...]
    codes = jnp.concatenate(
        [ref[k, 16, 0:1, :pick.shape[1]].astype(F32) for ref in (near_ref, far_ref) for k in range(4)],
        axis=0,
    )
    code_slot = nt(codes.astype(BF16), pick)
    layers = code_slot.shape[0]
    signs = expert_signs(code_slot)
    layer = jnp.concatenate([jnp.full((1, 8, slots), d, jnp.int32) for d in LAYER_ORDER]) ^ me
    signs = jnp.where(layer > me, signs, 0.0)
    signs_ref[...] = signs
    filled = nt(jnp.ones((8, pick.shape[1]), BF16), pick)
    apart = jnp.zeros((8, slots), F32)
    for block in (a0, a1, a2, a3):
        for k in range(4):
            apart += block[k, slots:slots + 8, :slots].astype(F32)
    gate = filled / (1.0 + jnp.exp(jnp.sum(apart, axis=0, keepdims=True)))
    gate_ref[...] = gate
    total = jnp.zeros((slots + layers * 8, hid_ref.shape[1]), F32)
    for far, block in enumerate((a0, a1, a2, a3)):
        for half in range(2):
            j = 4 * far + 2 * half
            left = jnp.concatenate([
                jnp.concatenate([block[2 * half + i, :slots] for i in range(2)], axis=1),
                jnp.concatenate(
                    [router_rows(near_ref, far_ref, ways[j + i]) for i in range(2)], axis=1
                ),
            ], axis=0)
            copies[j].wait()
            copies[j + 1].wait()
            total += nn(left, wbuf[j // 2])
    product, mixed = total[:slots], total[slots:].astype(BF16)
    product_ref[...] = product
    mixed_ref[...] = mixed
    hid = hid_ref[...]
    base = jnp.sum(hid.astype(F32) * product, axis=1, keepdims=True)
    base = jnp.sum(diagonal(slots) * base, axis=0, keepdims=True)
    cross = nt(mixed, hid).reshape(signs.shape)
    coefs = jnp.sum(signs * cross, axis=1)
    table = jnp.where(iota((layers, slots), 0) == 0, base, coefs) * (gate * (1.0 - gate))
    table_ref[...] = jnp.broadcast_to(table.astype(BF16)[None], table_ref.shape)


def side_kernel(here_ref, a0, a1, a2, a3, near_ref, far_ref, hid_ref, gate_ref,
                left_ref, picks_ref, scaled_ref, local_ref, codes_ref, *, tok, cap):
    slots, width = hid_ref.shape[0], a0.shape[2]
    me, at = here_ref[0], here_ref[1]
    codes = jnp.concatenate(
        [ref[k, 16, 0:1, :codes_ref.shape[1]].astype(F32) for ref in (near_ref, far_ref) for k in range(4)],
        axis=0,
    )
    codes_ref[...] = codes
    slot = slot_of(codes, tok, cap)
    for i, d in enumerate(LAYER_ORDER):
        pick = (iota((slots, slot.shape[1]), 0) == slot[i:i + 1]).astype(F32).astype(BF16)
        picks_ref[me ^ d] = pick
    gate_col = jnp.sum(diagonal(slots) * gate_ref[0:1], axis=1, keepdims=True)
    scaled_ref[...] = (gate_col * hid_ref[...].astype(F32)).astype(BF16)
    local_ref[...] = router_rows(near_ref, far_ref, at)
    for far, block in enumerate((a0, a1, a2, a3)):
        for k in range(4):
            way = block_way(at, (me & 1) == 1, far, k)
            left_ref[pl.ds((4 * far + k) * width, width), :] = jnp.concatenate(
                [block[k, :slots], router_rows(near_ref, far_ref, way)], axis=0
            ).T


def tail_kernel(here_ref, got_ref, picks_ref, codes_ref, pick_ref, signs_ref, gate_ref,
                product_ref, mixed_ref, scaled_ref, left_ref, x_ref, local_ref, grads_ref,
                input_ref, hidden_ref, down_ref, router_ref,
                delta_ref, step_ref, ibuf, isems, obuf, sems):
    layers, slots = codes_ref.shape[0], gate_ref.shape[1]
    tokens, width = codes_ref.shape[1], x_ref.shape[1]
    ways = got_ref.shape[0] // layers
    loads = [
        pltpu.make_async_copy(left_ref.at[pl.ds(j * width, width)], ibuf.at[j], isems.at[j])
        for j in range(ways)
    ]
    for load in loads:
        load.start()
    me, at = here_ref[0], here_ref[1]
    rows = []
    for s in range(layers):
        table = got_ref[s * ways].astype(F32)
        for p in range(1, ways):
            table += got_ref[s * ways + p].astype(F32)
        first = table.astype(BF16)
        rest = table - first.astype(F32)
        second = rest.astype(BF16)
        third = (rest - second.astype(F32)).astype(BF16)
        parts = nn(jnp.concatenate([first, second, third], axis=0), picks_ref[s])
        rows.append(parts[:8] + parts[8:16] + parts[16:])
    deltas = [None] * layers
    for layer in range(layers - 1, -1, -1):
        value = rows[layer][0:1]
        for upper in range(layer + 1, layers):
            i = LAYER_ORDER.index(layer ^ upper)
            value += deltas[upper] * rows[layer][i:i + 1]
        deltas[layer] = value.astype(BF16).astype(F32)
        delta_ref[layer:layer + 1, :] = deltas[layer]
    mine = jnp.concatenate([delta_ref[pl.ds(me ^ d, 1), :] for d in LAYER_ORDER], axis=0)
    delta_slot = nt(mine.astype(BF16), pick_ref[...])
    lift = (signs_ref[...] * delta_slot[:, None, :]).reshape(layers * 8, slots).astype(BF16)
    scaled = scaled_ref[...]
    right = jnp.concatenate([scaled, nn(lift, scaled).astype(BF16)], axis=0)
    copies = []
    for j in range(ways):
        way = block_way(at, (me & 1) == 1, j // 4, j % 4)
        loads[j].wait()
        obuf[j] = nn(ibuf[j], right).astype(BF16)
        copies.append(
            pltpu.make_async_copy(
                obuf.at[j],
                down_ref.at[pl.ds(pl.multiple_of(way * width, width), width)],
                sems.at[j],
            )
        )
        copies[-1].start()
    gate_col = jnp.sum(diagonal(slots) * gate_ref[0:1], axis=1, keepdims=True)
    hidden_ref[...] = (gate_col * (product_ref[...] + tn(lift, mixed_ref[...]))).astype(BF16)
    logit_grads = expert_signs(codes_ref[...]) * mine[:, None, :]
    router_ref[...] = nn(logit_grads[0].astype(BF16), x_ref[...])
    step_ref[...] = tn(logit_grads.reshape(layers * 8, tokens).astype(BF16), local_ref[...])
    count = grads_ref.shape[0]
    tok = tokens // count
    own = grads_ref.shape[1]
    for m in range(count):
        step = step_ref[pl.ds(pl.multiple_of(m * tok + me * own, 8), own), :]
        input_ref[m] = (grads_ref[m].astype(F32) + step).astype(BF16)
    for copy in copies:
        copy.wait()


def call(kernel, outs, in_specs, scratch, limit, out_specs=None, flops=0, moved=0):
    return pl.pallas_call(
        kernel,
        out_shape=[jax.ShapeDtypeStruct(*o) for o in outs],
        in_specs=in_specs,
        out_specs=out_specs or [AUTO] * len(outs),
        scratch_shapes=scratch,
        compiler_params=pltpu.CompilerParams(vmem_limit_bytes=limit << 20),
        cost_estimate=pl.CostEstimate(flops=flops, bytes_accessed=moved, transcendentals=0),
    )


def per_device(layer_inputs, expert_ids, hidden, down_weight, router_weight, grad_out):
    sections, ways = lax.axis_size("section"), lax.axis_size("dp")
    me, at = lax.axis_index("section"), lax.axis_index("dp")
    micro, tok, width = grad_out.shape
    cap, units = hidden.shape[2:]
    experts = router_weight.shape[2]
    tokens, slots = micro * tok, micro * cap
    full = ways * width
    x = layer_inputs[0].reshape(tokens, width)
    ids = expert_ids[0].reshape(tokens, 2)
    hid = hidden[0].reshape(slots, units)
    router = router_weight[0].T
    grads = grad_out.reshape(tokens, width)

    got_router = to_all(router, "dp", ways)

    other = jnp.where(ids[:, 0] == 0, ids[:, 1], ids[:, 0])
    member = (ids[:, 0] == 0) | (ids[:, 1] == 0)
    code = jnp.where(member, other, 0).astype(F32)
    code_block = jnp.zeros((1, experts, width), BF16).at[0, 0, :tokens].set(code.astype(BF16))
    slot = slot_of(code[None], tok, cap)
    pick = (slot == iota((slots, 1), 0)).astype(BF16)
    apart = -jnp.sum(expert_signs(code[None])[0] * nt(router, x), axis=0)
    parts = jnp.stack(pieces(apart))
    parts = jnp.pad(nt(parts, pick).astype(BF16), ((0, 8 - 3), (0, width - slots)))
    rows = nn(pick, grads).astype(BF16)
    block = jnp.concatenate([rows, parts])

    group = jnp.stack([block] + [turn(block, 0, step) for step in (1, 2, 3)])
    blocks = [group] + [turn(group, 1, step) for step in (1, 2, 3)]
    mine = jnp.concatenate([got_router, code_block])
    near = jnp.stack([mine] + [swap(mine, "section", d) for d in SECTION_STEPS])
    far = swap(near, "section", 1)
    own = tok // sections
    grads_mine = lax.dynamic_slice_in_dim(grad_out, me * own, own, axis=1)
    place = jnp.stack([me, at]).astype(jnp.int32)

    table, product, mixed, signs, gate = call(
        mid_kernel,
        [
            ((sections * ways, sections, slots), BF16),
            ((slots, units), F32),
            ((sections * experts, units), BF16),
            ((sections, experts, slots), F32),
            ((8, slots), F32),
        ],
        [SMEM] + [AUTO] * 8 + [HBM],
        [pltpu.VMEM((ways // 2, 2 * width, units), BF16), pltpu.SemaphoreType.DMA((ways,))],
        60,
        flops=2 * 192 * full * units,
        moved=full * units * 2,
    )(place, *blocks, near, far, hid, pick, down_weight[0])

    got_table = lax.all_to_all(table, ("section", "dp"), 0, 0, tiled=True)

    left, picks, scaled, local, codes = call(
        lambda *refs: side_kernel(*refs, tok=tok, cap=cap),
        [
            ((full, slots + sections * experts), BF16),
            ((sections, slots, tokens), BF16),
            ((slots, units), BF16),
            ((sections * experts, width), BF16),
            ((sections, tokens), F32),
        ],
        [SMEM] + [AUTO] * 8,
        [],
        60,
        flops=10**9,
        moved=4 * full * 192,
    )(place, *blocks, near, far, hid, gate)

    input_grad, hidden_grad, down_grad, router_grad = call(
        tail_kernel,
        [
            ((micro, own, width), BF16),
            ((slots, units), BF16),
            ((full, units), BF16),
            ((experts, width), F32),
        ],
        [SMEM] + [AUTO] * 9 + [HBM] + [AUTO] * 3,
        [
            pltpu.VMEM((sections, tokens), F32),
            pltpu.VMEM((tokens, width), F32),
            pltpu.VMEM((ways, width, slots + sections * experts), BF16),
            pltpu.SemaphoreType.DMA((ways,)),
            pltpu.VMEM((ways, width, units), BF16),
            pltpu.SemaphoreType.DMA((ways,)),
        ],
        60,
        out_specs=[AUTO, AUTO, HBM, AUTO],
        flops=2 * 192 * full * units,
        moved=full * units * 2,
    )(
        place, got_table, picks, codes, pick, signs, gate,
        product, mixed, scaled, left, x, local, grads_mine,
    )
    return (
        input_grad,
        hidden_grad.reshape(1, micro, cap, units),
        down_grad[None],
        router_grad.T[None],
    )


def solution(mesh):
    return jax.shard_map(
        per_device,
        mesh=mesh,
        in_specs=(
            P("section", None, None, "dp"),
            P("section", None, None, None),
            P("section", None, None, "dp"),
            P("section", None, "dp"),
            P("section", "dp", None),
            P(None, None, "dp"),
        ),
        out_specs=(
            P(None, "section", "dp"),
            P("section", None, None, "dp"),
            P("section", None, "dp"),
            P("section", "dp", None),
        ),
        check_vma=False,
    )
```

```python
import jax
import jax.numpy as jnp
from jax import lax
from jax.experimental import pallas as pl
from jax.experimental.pallas import tpu as pltpu
from jax.sharding import PartitionSpec as P

F32 = jnp.float32
BF16 = jnp.bfloat16
HBM = pl.BlockSpec(memory_space=pltpu.HBM)
GRANT = 62 << 20
RING = (0, 1, 3, 2)
SECTION_STEPS = (2, 6, 4)
LAYER_ORDER = [d ^ core for core in (0, 1) for d in (0,) + SECTION_STEPS]


def nt(a, b):
    return lax.dot_general(a, b, (((1,), (1,)), ((), ())), preferred_element_type=F32)


def tn(a, b):
    return lax.dot_general(a, b, (((0,), (0,)), ((), ())), preferred_element_type=F32)


def nn(a, b):
    return jnp.dot(a, b, preferred_element_type=F32)


def swap(value, axis, distance):
    count = lax.axis_size(axis)
    return lax.ppermute(value, axis, [(i, i ^ distance) for i in range(count)])


def turn(value, stage, step):
    sections, ways = lax.axis_size("section"), lax.axis_size("dp")
    pairs = []
    for s in range(sections):
        distance = RING[step] * (1 if s % 2 == stage else 4)
        pairs += [(s * ways + p, s * ways + (p ^ distance)) for p in range(ways)]
    return lax.ppermute(value, ("section", "dp"), pairs)


def iota(shape, dim):
    return lax.broadcasted_iota(jnp.int32, shape, dim)


def slot_of(codes, tok, cap):
    tokens = codes.shape[1]
    row, col = iota((tokens, tokens), 0), iota((tokens, tokens), 1)
    before = ((row < col) & (row // tok == col // tok)).astype(F32).astype(BF16)
    member = codes > 0.0
    rank = nn(member.astype(F32).astype(BF16), before).astype(jnp.int32)
    return jnp.where(member, rank + (iota(codes.shape, 1) // tok) * cap, -1)


def expert_signs(codes):
    experts = iota((codes.shape[0], 8, codes.shape[1]), 1).astype(F32)
    return (experts == 0.0).astype(F32) - (experts == codes[:, None, :]).astype(F32)


def diagonal(size):
    return (iota((size, size), 0) == iota((size, size), 1)).astype(F32)


def block_of(at, odd, way):
    apart = at ^ way
    low, high = apart & 3, apart >> 2
    low, high = low ^ (low >> 1), high ^ (high >> 1)
    return jnp.where(odd, 4 * low + high, 4 * high + low)


def left_block(rows, near, far, j, slots):
    turned = 4 * (j & 3) + (j >> 2)
    size = slots + 16
    members = rows[pl.ds(pl.multiple_of(j * size, 16), slots), :]
    routers = [near[17 * k + j] for k in range(4)] + [far[17 * k + turned] for k in range(4)]
    return jnp.concatenate([members] + routers, axis=0)


def layer_codes(near, far, tokens):
    return jnp.concatenate(
        [ref[17 * k + 16, 0:1, :tokens].astype(F32) for ref in (near, far) for k in range(4)],
        axis=0,
    )


def split(value):
    first = value.astype(BF16)
    rest = value - first.astype(F32)
    second = rest.astype(BF16)
    return [first, second, (rest - second.astype(F32)).astype(BF16)]


def pre_kernel(ins, raws, outs, raw_outs, *, cap):
    ids, grads, x, router = ins
    block, pick_out, code_out, mine_out = outs
    slots, tokens = pick_out.ref.shape
    tok = ids.ref.shape[1]
    micro = tokens // tok
    left = jnp.concatenate([ids.ref[2 * m:2 * m + 1, :] for m in range(micro)], axis=1)
    right = jnp.concatenate([ids.ref[2 * m + 1:2 * m + 2, :] for m in range(micro)], axis=1)
    code = jnp.where(left == 0, right, jnp.where(right == 0, left, 0)).astype(F32)
    code = jnp.broadcast_to(code, (16, tokens))
    code_out.ref[...] = jnp.zeros(code_out.ref.shape, BF16)
    code_out.ref[:, :tokens] = code.astype(BF16)
    code_out.flush()
    slot = slot_of(code[:8], tok, cap)[0:1]
    pick = (iota((slots, tokens), 0) == slot).astype(F32).astype(BF16)
    pick_out.ref[...] = pick
    pick_out.flush()
    block.ref[:slots, :] = nn(pick, grads.ref[...]).astype(BF16)
    me, _, _ = place()
    count = mine_out.ref.shape[0]
    own = count // micro
    wanted = iota((count, 1), 0)
    wanted = (wanted // own) * tok + me * own + wanted % own
    choose = (iota((count, tokens), 1) == wanted).astype(F32).astype(BF16)
    mine_out.ref[...] = nn(choose, grads.ref[...]).astype(BF16)
    mine_out.flush()
    logits = nt(router.ref[...], x.ref[...])
    apart = -jnp.sum(expert_signs(code[0:1])[0] * logits, axis=0, keepdims=True)
    parts = jnp.concatenate(split(apart) + [jnp.zeros((5, tokens), BF16)], axis=0)
    parts = jnp.concatenate(
        [nt(parts, pick), jnp.zeros((8, block.ref.shape[1] - slots), F32)], axis=1
    )
    both = jnp.concatenate([router.ref[...].astype(F32), parts], axis=0)
    block.ref[slots:, :] = both.astype(BF16)


def logit_parts(rows, slots, ways):
    apart = jnp.zeros((8, slots), F32)
    for j in range(ways):
        at = j * (slots + 16) + slots
        apart += rows[at:at + 16, :slots].astype(F32)[8:]
    return apart


def mid_kernel(ins, raws, outs, raw_outs, rows, wbuf, sems):
    hid, pick, near, far = ins
    blocks, w_ref = raws[:4], raws[4]
    table_out, product_out, mixed_out, signs_out, gate_out = outs
    slots, width = hid.buffer.shape[0], near.buffer.shape[2]
    size = blocks[0].shape[0]
    ways = wbuf.shape[0] // width
    loads = [
        pltpu.make_async_copy(block, rows.at[pl.ds(n * size, size)], sems.at[n])
        for n, block in enumerate(blocks)
    ]
    depth = wbuf.shape[0] // 4
    loads += [
        pltpu.make_async_copy(
            w_ref.at[pl.ds(q * depth, depth)], wbuf.at[pl.ds(q * depth, depth)], sems.at[4 + q]
        )
        for q in range(4)
    ]
    for load in loads:
        load.start()
    me, at, odd = place()
    codes = layer_codes(near.ref, far.ref, pick.ref.shape[1])
    signs = expert_signs(nt(codes.astype(BF16), pick.ref[...]))
    layer = jnp.concatenate([jnp.full((1, 8, slots), d, jnp.int32) for d in LAYER_ORDER]) ^ me
    signs = jnp.where(layer > me, signs, 0.0)
    signs_out.ref[...] = signs
    filled = nt(jnp.ones((8, pick.buffer.shape[1]), BF16), pick.ref[...])
    for load in loads[:4]:
        load.wait()
    apart = jnp.sum(logit_parts(rows, slots, ways), axis=0, keepdims=True)
    gate = filled / (1.0 + jnp.exp(apart))
    gate_out.ref[...] = gate
    slope = gate * (1.0 - gate)
    total = jnp.zeros((slots + mixed_out.ref.shape[0], mixed_out.ref.shape[1]), F32)
    for way in range(0, ways, 2):
        left = jnp.concatenate([
            left_block(rows, near.ref, far.ref, block_of(at, odd, way + i), slots)
            for i in range(2)
        ], axis=1)
        if way % 4 == 0:
            loads[4 + way // 4].wait()
        total += nn(left, wbuf[way * width:(way + 2) * width])
    product, mixed = total[:slots], total[slots:].astype(BF16)
    base = jnp.sum(hid.ref[...].astype(F32) * product, axis=1, keepdims=True)
    base = jnp.sum(diagonal(slots) * base, axis=0, keepdims=True)
    cross = nt(mixed, hid.ref[...]).reshape(signs.shape)
    coefs = jnp.sum(signs * cross, axis=1)
    table = jnp.where(iota(coefs.shape, 0) == 0, base, coefs) * slope
    table = jnp.concatenate([table.astype(BF16)] * 2, axis=0)
    table_out.ref[...] = jnp.broadcast_to(table[None], table_out.ref.shape)
    table_out.flush()
    product_out.ref[...] = product
    mixed_out.ref[...] = mixed


def side_kernel(ins, raws, outs, raw_outs, *, tok, cap):
    near, far, hid, gate = ins
    picks_out, scaled_out, codes_out = outs
    slots = hid.buffer.shape[0]
    me, _, _ = place()
    codes = layer_codes(near.ref, far.ref, codes_out.ref.shape[1])
    codes_out.ref[...] = codes
    slot = slot_of(codes, tok, cap)
    for i, d in enumerate(LAYER_ORDER):
        pick = (iota((slots, slot.shape[1]), 0) == slot[i:i + 1]).astype(F32).astype(BF16)
        picks_out.ref[me ^ d] = pick
    gate_col = jnp.sum(diagonal(slots) * gate.ref[0:1], axis=1, keepdims=True)
    scaled_out.ref[...] = (gate_col * hid.ref[...].astype(F32)).astype(BF16)


def tail_kernel(ins, raws, outs, raw_outs, delta_ref, step_ref, rows, lsems, obuf, sems):
    got, picks, codes, signs, pick, scaled_in, near, far, product, mixed, gate, x, grads = ins
    blocks, down_ref = raws, raw_outs[0]
    input_out, hidden_out, router_out = outs
    layers, slots = codes.buffer.shape[0], gate.buffer.shape[1]
    tokens, width = codes.buffer.shape[1], x.buffer.shape[1]
    ways = obuf.shape[0] // width
    size = blocks[0].shape[0]
    loads = [
        pltpu.make_async_copy(block, rows.at[pl.ds(n * size, size)], lsems.at[n])
        for n, block in enumerate(blocks)
    ]
    for load in loads:
        load.start()
    me, at, odd = place()
    parts_of = []
    for s in range(layers):
        n = s * ways * 8
        table = jnp.sum(
            got.ref[n:n + ways * 8].astype(F32).reshape(ways, 8, slots), axis=0
        )
        parts = nn(jnp.concatenate(split(table), axis=0), picks.ref[s])
        parts_of.append(parts[:8] + parts[8:16] + parts[16:])
    deltas = [None] * layers
    for layer in range(layers - 1, -1, -1):
        value = parts_of[layer][0:1]
        for upper in range(layer + 1, layers):
            i = LAYER_ORDER.index(layer ^ upper)
            value += deltas[upper] * parts_of[layer][i:i + 1]
        deltas[layer] = value.astype(BF16).astype(F32)
        delta_ref[layer:layer + 1, :] = deltas[layer]
    mine = jnp.concatenate([delta_ref[pl.ds(me ^ d, 1), :] for d in LAYER_ORDER], axis=0)
    delta_slot = nt(mine.astype(BF16), pick.ref[...])
    lift = (signs.ref[...] * delta_slot[:, None, :]).reshape(layers * 8, slots).astype(BF16)
    scaled = scaled_in.ref[...]
    right = jnp.concatenate([scaled, nn(lift, scaled).astype(BF16)], axis=0)
    for load in loads:
        load.wait()
    copies = []
    for way in range(ways):
        left = left_block(rows, near.ref, far.ref, block_of(at, odd, way), slots)
        obuf[way * width:(way + 1) * width] = tn(left, right).astype(BF16)
        if way % 2 == 1:
            done = pl.ds((way - 1) * width, 2 * width)
            copies.append(
                pltpu.make_async_copy(obuf.at[done], down_ref.at[done], sems.at[way // 2])
            )
            copies[-1].start()
    gate_col = jnp.sum(diagonal(slots) * gate.ref[0:1], axis=1, keepdims=True)
    hidden = product.ref[...] + tn(lift, mixed.ref[...])
    hidden_out.ref[...] = (gate_col * hidden).astype(BF16)
    hidden_out.flush()
    logit_grads = expert_signs(codes.ref[...]) * mine[:, None, :]
    router_out.ref[...] = nn(logit_grads[0].astype(BF16), x.ref[...])
    router_out.flush()
    local = jnp.concatenate([ref[17 * k] for ref in (near.ref, far.ref) for k in range(4)], axis=0)
    step_ref[...] = tn(logit_grads.reshape(layers * 8, tokens).astype(BF16), local)
    count = 4
    own, tok = grads.buffer.shape[0] // count, tokens // count
    steps = jnp.concatenate([
        step_ref[pl.ds(pl.multiple_of(m * tok + me * own, 8), own), :] for m in range(count)
    ], axis=0)
    input_out.ref[...] = (grads.ref[...].astype(F32) + steps).astype(BF16)
    input_out.flush()
    for copy in copies:
        copy.wait()


class Staged:
    def __init__(self, source, buffer, semaphore):
        self.copy = pltpu.make_async_copy(source, buffer, semaphore)
        self.copy.start()
        self.buffer, self.waited = buffer, False

    @property
    def ref(self):
        if not self.waited:
            self.copy.wait()
            self.waited = True
        return self.buffer


class Result:
    def __init__(self, buffer, target, semaphore):
        self.ref, self.copy, self.sent = buffer, None, False
        self.parts = (buffer, target, semaphore)

    def flush(self):
        if not self.sent:
            self.copy = pltpu.make_async_copy(*self.parts)
            self.copy.start()
            self.sent = True


def call(kernel, staged, raw, results, raw_results=(), scratch=(), flops=0, moved=0):
    counts = (len(staged), len(raw), len(results), len(raw_results))

    def body(*refs):
        groups, at = [], 0
        for count in counts + (counts[0], counts[2]):
            groups.append(refs[at:at + count])
            at += count
        sources, raws, targets, raw_targets, ibufs, obufs = groups
        sems, rest = refs[at], refs[at + 1:]
        ins = [Staged(r, v, sems.at[n]) for n, (r, v) in enumerate(zip(sources, ibufs))]
        outs = [
            Result(v, r, sems.at[counts[0] + n]) for n, (r, v) in enumerate(zip(targets, obufs))
        ]
        kernel(ins, raws, outs, raw_targets, *rest)
        for item in ins:
            item.ref
        for item in outs:
            item.flush()
        for item in outs:
            item.copy.wait()

    shapes = [jax.ShapeDtypeStruct(*o) for o in results] + [
        jax.ShapeDtypeStruct(*o) for o in raw_results
    ]
    return pl.pallas_call(
        body,
        out_shape=shapes,
        in_specs=[HBM] * (counts[0] + counts[1]),
        out_specs=[HBM] * len(shapes),
        scratch_shapes=[pltpu.VMEM(v.shape, v.dtype) for v in staged]
        + [pltpu.VMEM(*o) for o in results]
        + [pltpu.SemaphoreType.DMA((counts[0] + counts[2],))]
        + list(scratch),
        compiler_params=pltpu.CompilerParams(vmem_limit_bytes=GRANT),
        cost_estimate=pl.CostEstimate(flops=flops, bytes_accessed=moved, transcendentals=0),
    )(*staged, *raw)


def place():
    me, at = lax.axis_index("section"), lax.axis_index("dp")
    return me, at, (me & 1) == 1


def per_device(layer_inputs, expert_ids, hidden, down_weight, router_weight, grad_out):
    sections, ways = lax.axis_size("section"), lax.axis_size("dp")
    micro, tok, width = grad_out.shape
    cap, units = hidden.shape[2:]
    experts = router_weight.shape[2]
    tokens, slots = micro * tok, micro * cap
    full = ways * width
    x = layer_inputs[0].reshape(tokens, width)
    hid = hidden[0].reshape(slots, units)
    router = router_weight[0].T
    grads = grad_out.reshape(tokens, width)

    own = tok // sections
    block, pick, code, grads_mine = call(
        lambda *refs: pre_kernel(*refs, cap=cap),
        [expert_ids[0].transpose(0, 2, 1).reshape(2 * micro, tok), grads, x, router],
        [],
        [((slots + 16, width), BF16), ((slots, tokens), BF16), ((16, width), BF16),
         ((micro * own, width), BF16)],
    )

    group = jnp.stack([block] + [turn(block, 0, step) for step in (1, 2, 3)])
    routers = group[:, slots:slots + experts]
    routers = [routers] + [turn(routers, 1, step) for step in (1, 2, 3)]
    blocks = [group] + [turn(group, 1, step) for step in (1, 2, 3)]
    blocks = [b.reshape(4 * (slots + 16), width) for b in blocks]
    mine = jnp.concatenate(routers + [code[None, :experts]])
    weights = down_weight[0]
    near = jnp.concatenate([mine] + [swap(mine, "section", d) for d in SECTION_STEPS])
    far = swap(near, "section", 1)

    rows_buffer = pltpu.VMEM((ways * (slots + 16), width), BF16)
    table, product, mixed, signs, gate = call(
        mid_kernel,
        [hid, pick, near, far],
        blocks + [weights],
        [
            ((sections * ways // 2, 2 * sections, slots), BF16),
            ((slots, units), F32),
            ((sections * experts, units), BF16),
            ((sections, experts, slots), F32),
            ((8, slots), F32),
        ],
        scratch=[rows_buffer, pltpu.VMEM((full, units), BF16), pltpu.SemaphoreType.DMA((8,))],
    )
    table = table.reshape(sections * ways, sections, slots)
    got_table = lax.all_to_all(table, ("section", "dp"), 0, 0, tiled=True)

    picks, scaled, codes = call(
        lambda *refs: side_kernel(*refs, tok=tok, cap=cap),
        [near, far, hid, gate],
        [],
        [
            ((sections, slots, tokens), BF16),
            ((slots, units), BF16),
            ((sections, tokens), F32),
        ],
        flops=10**9,
        moved=10**7,
    )
    input_grad, hidden_grad, router_grad, down_grad = call(
        tail_kernel,
        [
            got_table.reshape(-1, slots), picks, codes, signs, pick, scaled, near, far,
            product, mixed, gate, x, grads_mine,
        ],
        blocks,
        [
            ((micro * own, width), BF16),
            ((slots, units), BF16),
            ((experts, width), F32),
        ],
        raw_results=[((full, units), BF16)],
        scratch=[
            pltpu.VMEM((sections, tokens), F32),
            pltpu.VMEM((tokens, width), F32),
            rows_buffer,
            pltpu.SemaphoreType.DMA((4,)),
            pltpu.VMEM((full, units), BF16),
            pltpu.SemaphoreType.DMA((ways // 2,)),
        ],
        flops=2 * 192 * full * units,
        moved=full * units * 2,
    )
    return (
        input_grad.reshape(micro, own, width),
        hidden_grad.reshape(1, micro, cap, units),
        down_grad[None],
        router_grad.T[None],
    )


def solution(mesh):
    return jax.shard_map(
        per_device,
        mesh=mesh,
        in_specs=(
            P("section", None, None, "dp"),
            P("section", None, None, None),
            P("section", None, None, "dp"),
            P("section", None, "dp"),
            P("section", "dp", None),
            P(None, None, "dp"),
        ),
        out_specs=(
            P(None, "section", "dp"),
            P("section", None, None, "dp"),
            P("section", None, "dp"),
            P("section", "dp", None),
        ),
        check_vma=False,
    )
```

```python
import jax
import jax.numpy as jnp
from jax import lax
from jax.experimental import pallas as pl
from jax.experimental.pallas import tpu as pltpu
from jax.sharding import PartitionSpec as P

F32 = jnp.float32
BF16 = jnp.bfloat16
HBM = pl.BlockSpec(memory_space=pltpu.HBM)
GRANT = 62 << 20
RING = (0, 1, 3, 2)
SECTION_STEPS = (2, 6, 4)
LAYER_ORDER = [d ^ core for core in (0, 1) for d in (0,) + SECTION_STEPS]


def nt(a, b):
    return lax.dot_general(a, b, (((1,), (1,)), ((), ())), preferred_element_type=F32)


def tn(a, b):
    return lax.dot_general(a, b, (((0,), (0,)), ((), ())), preferred_element_type=F32)


def nn(a, b):
    return jnp.dot(a, b, preferred_element_type=F32)


def swap(value, axis, distance):
    count = lax.axis_size(axis)
    return lax.ppermute(value, axis, [(i, i ^ distance) for i in range(count)])


def turn(value, stage, step):
    sections, ways = lax.axis_size("section"), lax.axis_size("dp")
    pairs = []
    for s in range(sections):
        distance = RING[step] * (1 if s % 2 == stage else 4)
        pairs += [(s * ways + p, s * ways + (p ^ distance)) for p in range(ways)]
    return lax.ppermute(value, ("section", "dp"), pairs)


def iota(shape, dim):
    return lax.broadcasted_iota(jnp.int32, shape, dim)


def slot_of(codes, tok, cap):
    tokens = codes.shape[1]
    row, col = iota((tokens, tokens), 0), iota((tokens, tokens), 1)
    before = ((row < col) & (row // tok == col // tok)).astype(F32).astype(BF16)
    member = codes > 0.0
    rank = nn(member.astype(F32).astype(BF16), before).astype(jnp.int32)
    return jnp.where(member, rank + (iota(codes.shape, 1) // tok) * cap, -1)


def expert_signs(codes):
    experts = iota((codes.shape[0], 8, codes.shape[1]), 1).astype(F32)
    return (experts == 0.0).astype(F32) - (experts == codes[:, None, :]).astype(F32)


def diagonal(size):
    return (iota((size, size), 0) == iota((size, size), 1)).astype(F32)


def block_of(at, odd, way):
    apart = at ^ way
    low, high = apart & 3, apart >> 2
    low, high = low ^ (low >> 1), high ^ (high >> 1)
    return jnp.where(odd, 4 * low + high, 4 * high + low)


def left_block(rows, near, far, j, slots):
    turned = 4 * (j & 3) + (j >> 2)
    size = slots + 16
    members = rows[pl.ds(pl.multiple_of(j * size, 16), slots), :]
    routers = [near[17 * k + j] for k in range(4)] + [far[17 * k + turned] for k in range(4)]
    return jnp.concatenate([members] + routers, axis=0)


def layer_codes(near, far, tokens):
    return jnp.concatenate(
        [ref[17 * k + 16, 0:1, :tokens].astype(F32) for ref in (near, far) for k in range(4)],
        axis=0,
    )


def split(value):
    first = value.astype(BF16)
    rest = value - first.astype(F32)
    second = rest.astype(BF16)
    return [first, second, (rest - second.astype(F32)).astype(BF16)]


def pre_kernel(ins, raws, outs, raw_outs, *, cap):
    ids, grads, x, router = ins
    block, pick_out, code_out, mine_out = outs
    slots, tokens = pick_out.ref.shape
    tok = ids.ref.shape[1]
    micro = tokens // tok
    left = jnp.concatenate([ids.ref[2 * m:2 * m + 1, :] for m in range(micro)], axis=1)
    right = jnp.concatenate([ids.ref[2 * m + 1:2 * m + 2, :] for m in range(micro)], axis=1)
    code = jnp.where(left == 0, right, jnp.where(right == 0, left, 0)).astype(F32)
    code = jnp.broadcast_to(code, (16, tokens))
    code_out.ref[...] = jnp.zeros(code_out.ref.shape, BF16)
    code_out.ref[:, :tokens] = code.astype(BF16)
    code_out.flush()
    slot = slot_of(code[:8], tok, cap)[0:1]
    pick = (iota((slots, tokens), 0) == slot).astype(F32).astype(BF16)
    pick_out.ref[...] = pick
    pick_out.flush()
    block.ref[:slots, :] = nn(pick, grads.ref[...]).astype(BF16)
    me, _, _ = place()
    count = mine_out.ref.shape[0]
    own = count // micro
    wanted = iota((count, 1), 0)
    wanted = (wanted // own) * tok + me * own + wanted % own
    choose = (iota((count, tokens), 1) == wanted).astype(F32).astype(BF16)
    mine_out.ref[...] = nn(choose, grads.ref[...]).astype(BF16)
    mine_out.flush()
    logits = nt(router.ref[...], x.ref[...])
    apart = -jnp.sum(expert_signs(code[0:1])[0] * logits, axis=0, keepdims=True)
    parts = jnp.concatenate(split(apart) + [jnp.zeros((5, tokens), BF16)], axis=0)
    parts = jnp.concatenate(
        [nt(parts, pick), jnp.zeros((8, block.ref.shape[1] - slots), F32)], axis=1
    )
    both = jnp.concatenate([router.ref[...].astype(F32), parts], axis=0)
    block.ref[slots:, :] = both.astype(BF16)


def logit_parts(rows, slots, ways):
    apart = jnp.zeros((8, slots), F32)
    for j in range(ways):
        at = j * (slots + 16) + slots
        apart += rows[at:at + 16, :slots].astype(F32)[8:]
    return apart


def load_weights(w_ref, wbuf, sems, first):
    count = sems.shape[0]
    depth = wbuf.shape[0] // count
    copies = [
        pltpu.make_async_copy(
            w_ref.at[pl.ds(first + q * depth, depth)], wbuf.at[pl.ds(q * depth, depth)], sems.at[q]
        )
        for q in range(count)
    ]
    for copy in copies:
        copy.start()
    return copies


def load_rows(blocks, rows, sems):
    size = blocks[0].shape[0]
    loads = [
        pltpu.make_async_copy(block, rows.at[pl.ds(n * size, size)], sems.at[n])
        for n, block in enumerate(blocks)
    ]
    for load in loads:
        load.start()
    return loads


def back_kernel(ins, raws, outs, raw_outs, wbuf, sems, *, first):
    hid, back = ins[0], outs[0]
    copies = load_weights(raws[0], wbuf, sems, first)
    depth = wbuf.shape[0] // len(copies)
    hidden = hid.ref[...].T
    for q, copy in enumerate(copies):
        copy.wait()
        for part in range(4):
            rows = pl.ds(q * depth + part * (depth // 4), depth // 4)
            back.ref[rows, :] = nn(wbuf[rows, :], hidden).astype(BF16)


def mid_kernel(ins, raws, outs, raw_outs, rows, sems):
    pick, near, far, low, high = ins
    table_out, signs_out, gate_out = outs
    slots, width = pick.buffer.shape[0], near.buffer.shape[2]
    loads = load_rows(raws, rows, sems)
    me, at, odd = place()
    codes = layer_codes(near.ref, far.ref, pick.ref.shape[1])
    signs = expert_signs(nt(codes.astype(BF16), pick.ref[...]))
    layer = jnp.concatenate([jnp.full((1, 8, slots), d, jnp.int32) for d in LAYER_ORDER]) ^ me
    signs = jnp.where(layer > me, signs, 0.0)
    signs_out.ref[...] = signs
    filled = nt(jnp.ones((8, pick.buffer.shape[1]), BF16), pick.ref[...])
    for load in loads:
        load.wait()
    halves = (low.ref, high.ref)
    ways = 2 * (low.buffer.shape[0] // width)
    apart = jnp.sum(logit_parts(rows, slots, ways), axis=0, keepdims=True)
    gate = filled / (1.0 + jnp.exp(apart))
    gate_out.ref[...] = gate
    slope = gate * (1.0 - gate)
    total = jnp.zeros((slots + signs.shape[0] * 8, slots), F32)
    for way in range(0, ways, 2):
        left = jnp.concatenate([
            left_block(rows, near.ref, far.ref, block_of(at, odd, way + i), slots)
            for i in range(2)
        ], axis=1)
        at_row = way % (ways // 2) * width
        total += nn(left, halves[way * 2 // ways][at_row:at_row + 2 * width])
    base = jnp.sum(diagonal(slots) * total[:slots], axis=0, keepdims=True)
    coefs = jnp.sum(signs * total[slots:].reshape(signs.shape), axis=1)
    table = jnp.where(iota(coefs.shape, 0) == 0, base, coefs) * slope
    table = jnp.concatenate([table.astype(BF16)] * 2, axis=0)
    table_out.ref[...] = jnp.broadcast_to(table[None], table_out.ref.shape)
    table_out.flush()


def side_kernel(ins, raws, outs, raw_outs, rows, lsems, wbuf, sems, *, tok, cap):
    near, far, hid, gate = ins
    picks_out, scaled_out, codes_out, product_out, mixed_out = outs
    slots, width = hid.buffer.shape[0], near.buffer.shape[2]
    loads = load_rows(raws[:4], rows, lsems)
    copies = load_weights(raws[4], wbuf, sems, 0)
    me, at, odd = place()
    codes = layer_codes(near.ref, far.ref, codes_out.ref.shape[1])
    codes_out.ref[...] = codes
    codes_out.flush()
    slot = slot_of(codes, tok, cap)
    for i, d in enumerate(LAYER_ORDER):
        pick = (iota((slots, slot.shape[1]), 0) == slot[i:i + 1]).astype(F32).astype(BF16)
        picks_out.ref[me ^ d] = pick
    picks_out.flush()
    gate_col = jnp.sum(diagonal(slots) * gate.ref[0:1], axis=1, keepdims=True)
    scaled_out.ref[...] = (gate_col * hid.ref[...].astype(F32)).astype(BF16)
    scaled_out.flush()
    for load in loads:
        load.wait()
    ways = wbuf.shape[0] // width
    total = jnp.zeros((slots + mixed_out.ref.shape[0], mixed_out.ref.shape[1]), F32)
    for way in range(0, ways, 2):
        left = jnp.concatenate([
            left_block(rows, near.ref, far.ref, block_of(at, odd, way + i), slots)
            for i in range(2)
        ], axis=1)
        if way * len(copies) % ways == 0:
            copies[way * len(copies) // ways].wait()
        total += nn(left, wbuf[way * width:(way + 2) * width])
    product_out.ref[...] = total[:slots]
    mixed_out.ref[...] = total[slots:].astype(BF16)


def tail_kernel(ins, raws, outs, raw_outs, delta_ref, step_ref, rows, lsems, obuf, sems):
    got, picks, codes, signs, pick, scaled_in, near, far, product, mixed, gate, x, grads = ins
    blocks, down_ref = raws, raw_outs[0]
    input_out, hidden_out, router_out = outs
    layers, slots = codes.buffer.shape[0], gate.buffer.shape[1]
    tokens, width = codes.buffer.shape[1], x.buffer.shape[1]
    ways = obuf.shape[0] // width
    loads = load_rows(blocks, rows, lsems)
    me, at, odd = place()
    parts_of = []
    for s in range(layers):
        n = s * ways * 8
        table = jnp.sum(
            got.ref[n:n + ways * 8].astype(F32).reshape(ways, 8, slots), axis=0
        )
        parts = nn(jnp.concatenate(split(table), axis=0), picks.ref[s])
        parts_of.append(parts[:8] + parts[8:16] + parts[16:])
    deltas = [None] * layers
    for layer in range(layers - 1, -1, -1):
        value = parts_of[layer][0:1]
        for upper in range(layer + 1, layers):
            i = LAYER_ORDER.index(layer ^ upper)
            value += deltas[upper] * parts_of[layer][i:i + 1]
        deltas[layer] = value.astype(BF16).astype(F32)
        delta_ref[layer:layer + 1, :] = deltas[layer]
    mine = jnp.concatenate([delta_ref[pl.ds(me ^ d, 1), :] for d in LAYER_ORDER], axis=0)
    delta_slot = nt(mine.astype(BF16), pick.ref[...])
    lift = (signs.ref[...] * delta_slot[:, None, :]).reshape(layers * 8, slots).astype(BF16)
    scaled = scaled_in.ref[...]
    right = jnp.concatenate([scaled, nn(lift, scaled).astype(BF16)], axis=0)
    for load in loads:
        load.wait()
    copies = []
    for way in range(ways):
        left = left_block(rows, near.ref, far.ref, block_of(at, odd, way), slots)
        obuf[way * width:(way + 1) * width] = tn(left, right).astype(BF16)
        if way % 2 == 1:
            done = pl.ds((way - 1) * width, 2 * width)
            copies.append(
                pltpu.make_async_copy(obuf.at[done], down_ref.at[done], sems.at[way // 2])
            )
            copies[-1].start()
    gate_col = jnp.sum(diagonal(slots) * gate.ref[0:1], axis=1, keepdims=True)
    hidden = product.ref[...] + tn(lift, mixed.ref[...])
    hidden_out.ref[...] = (gate_col * hidden).astype(BF16)
    hidden_out.flush()
    logit_grads = expert_signs(codes.ref[...]) * mine[:, None, :]
    router_out.ref[...] = nn(logit_grads[0].astype(BF16), x.ref[...])
    router_out.flush()
    local = jnp.concatenate([ref[17 * k] for ref in (near.ref, far.ref) for k in range(4)], axis=0)
    step_ref[...] = tn(logit_grads.reshape(layers * 8, tokens).astype(BF16), local)
    count = 4
    own, tok = grads.buffer.shape[0] // count, tokens // count
    steps = jnp.concatenate([
        step_ref[pl.ds(pl.multiple_of(m * tok + me * own, 8), own), :] for m in range(count)
    ], axis=0)
    input_out.ref[...] = (grads.ref[...].astype(F32) + steps).astype(BF16)
    input_out.flush()
    for copy in copies:
        copy.wait()


class Staged:
    def __init__(self, source, buffer, semaphore):
        self.copy = pltpu.make_async_copy(source, buffer, semaphore)
        self.copy.start()
        self.buffer, self.waited = buffer, False

    @property
    def ref(self):
        if not self.waited:
            self.copy.wait()
            self.waited = True
        return self.buffer


class Result:
    def __init__(self, buffer, target, semaphore):
        self.ref, self.copy, self.sent = buffer, None, False
        self.parts = (buffer, target, semaphore)

    def flush(self):
        if not self.sent:
            self.copy = pltpu.make_async_copy(*self.parts)
            self.copy.start()
            self.sent = True


def call(kernel, staged, raw, results, raw_results=(), scratch=(), flops=0, moved=0):
    counts = (len(staged), len(raw), len(results), len(raw_results))

    def body(*refs):
        groups, at = [], 0
        for count in counts + (counts[0], counts[2]):
            groups.append(refs[at:at + count])
            at += count
        sources, raws, targets, raw_targets, ibufs, obufs = groups
        sems, rest = refs[at], refs[at + 1:]
        ins = [Staged(r, v, sems.at[n]) for n, (r, v) in enumerate(zip(sources, ibufs))]
        outs = [
            Result(v, r, sems.at[counts[0] + n]) for n, (r, v) in enumerate(zip(targets, obufs))
        ]
        kernel(ins, raws, outs, raw_targets, *rest)
        for item in ins:
            item.ref
        for item in outs:
            item.flush()
        for item in outs:
            item.copy.wait()

    shapes = [jax.ShapeDtypeStruct(*o) for o in results] + [
        jax.ShapeDtypeStruct(*o) for o in raw_results
    ]
    return pl.pallas_call(
        body,
        out_shape=shapes,
        in_specs=[HBM] * (counts[0] + counts[1]),
        out_specs=[HBM] * len(shapes),
        scratch_shapes=[pltpu.VMEM(v.shape, v.dtype) for v in staged]
        + [pltpu.VMEM(*o) for o in results]
        + [pltpu.SemaphoreType.DMA((counts[0] + counts[2],))]
        + list(scratch),
        compiler_params=pltpu.CompilerParams(vmem_limit_bytes=GRANT),
        cost_estimate=pl.CostEstimate(flops=flops, bytes_accessed=moved, transcendentals=0),
    )(*staged, *raw)


def place():
    me, at = lax.axis_index("section"), lax.axis_index("dp")
    return me, at, (me & 1) == 1


def per_device(layer_inputs, expert_ids, hidden, down_weight, router_weight, grad_out):
    sections, ways = lax.axis_size("section"), lax.axis_size("dp")
    micro, tok, width = grad_out.shape
    cap, units = hidden.shape[2:]
    experts = router_weight.shape[2]
    tokens, slots = micro * tok, micro * cap
    full = ways * width
    x = layer_inputs[0].reshape(tokens, width)
    hid = hidden[0].reshape(slots, units)
    router = router_weight[0].T
    grads = grad_out.reshape(tokens, width)

    own = tok // sections
    block, pick, code, grads_mine = call(
        lambda *refs: pre_kernel(*refs, cap=cap),
        [expert_ids[0].transpose(0, 2, 1).reshape(2 * micro, tok), grads, x, router],
        [],
        [((slots + 16, width), BF16), ((slots, tokens), BF16), ((16, width), BF16),
         ((micro * own, width), BF16)],
    )

    weights = down_weight[0]

    def back(after, first):
        after, hid_after = lax.optimization_barrier((after, hid))
        return after, call(
            lambda *refs: back_kernel(*refs, first=first),
            [hid_after],
            [weights],
            [((full // 2, slots), BF16)],
            scratch=[pltpu.VMEM((full // 2, units), BF16), pltpu.SemaphoreType.DMA((2,))],
            moved=full * units,
        )[0]

    block, low = back(block, 0)
    group = [block] + [turn(block, 0, step) for step in (1, 2, 3)]
    group, low = lax.optimization_barrier((group, low))
    group = jnp.stack(group)
    routers, high = back(group[:, slots:slots + experts], full // 2)
    routers = [routers] + [turn(routers, 1, step) for step in (1, 2, 3)]
    routers, high = lax.optimization_barrier((routers, high))
    blocks = [group] + [turn(group, 1, step) for step in (1, 2, 3)]
    blocks = [b.reshape(4 * (slots + 16), width) for b in blocks]
    mine = jnp.concatenate(routers + [code[None, :experts]])
    near = jnp.concatenate([mine] + [swap(mine, "section", d) for d in SECTION_STEPS])
    far = swap(near, "section", 1)

    rows_buffer = pltpu.VMEM((ways * (slots + 16), width), BF16)
    table, signs, gate = call(
        mid_kernel,
        [pick, near, far, low, high],
        blocks,
        [
            ((sections * ways // 2, 2 * sections, slots), BF16),
            ((sections, experts, slots), F32),
            ((8, slots), F32),
        ],
        scratch=[rows_buffer, pltpu.SemaphoreType.DMA((4,))],
    )
    table = table.reshape(sections * ways, sections, slots)
    got_table = lax.all_to_all(table, ("section", "dp"), 0, 0, tiled=True)

    picks, scaled, codes, product, mixed = call(
        lambda *refs: side_kernel(*refs, tok=tok, cap=cap),
        [near, far, hid, gate],
        blocks + [weights],
        [
            ((sections, slots, tokens), BF16),
            ((slots, units), BF16),
            ((sections, tokens), F32),
            ((slots, units), F32),
            ((sections * experts, units), BF16),
        ],
        scratch=[
            rows_buffer,
            pltpu.SemaphoreType.DMA((4,)),
            pltpu.VMEM((full, units), BF16),
            pltpu.SemaphoreType.DMA((4,)),
        ],
        flops=10**9,
        moved=10**7,
    )
    input_grad, hidden_grad, router_grad, down_grad = call(
        tail_kernel,
        [
            got_table.reshape(-1, slots), picks, codes, signs, pick, scaled, near, far,
            product, mixed, gate, x, grads_mine,
        ],
        blocks,
        [
            ((micro * own, width), BF16),
            ((slots, units), BF16),
            ((experts, width), F32),
        ],
        raw_results=[((full, units), BF16)],
        scratch=[
            pltpu.VMEM((sections, tokens), F32),
            pltpu.VMEM((tokens, width), F32),
            rows_buffer,
            pltpu.SemaphoreType.DMA((4,)),
            pltpu.VMEM((full, units), BF16),
            pltpu.SemaphoreType.DMA((ways // 2,)),
        ],
        flops=2 * 192 * full * units,
        moved=full * units * 2,
    )
    return (
        input_grad.reshape(micro, own, width),
        hidden_grad.reshape(1, micro, cap, units),
        down_grad[None],
        router_grad.T[None],
    )


def solution(mesh):
    return jax.shard_map(
        per_device,
        mesh=mesh,
        in_specs=(
            P("section", None, None, "dp"),
            P("section", None, None, None),
            P("section", None, None, "dp"),
            P("section", None, "dp"),
            P("section", "dp", None),
            P(None, None, "dp"),
        ),
        out_specs=(
            P(None, "section", "dp"),
            P("section", None, None, "dp"),
            P("section", None, "dp"),
            P("section", "dp", None),
        ),
        check_vma=False,
    )
```

```python
import jax
import jax.numpy as jnp
from jax import lax
from jax.experimental import pallas as pl
from jax.experimental.pallas import tpu as pltpu
from jax.sharding import PartitionSpec as P

F32 = jnp.float32
BF16 = jnp.bfloat16
HBM = pl.BlockSpec(memory_space=pltpu.HBM)
GRANT = 62 << 20
RING = (0, 1, 3, 2)
SECTION_STEPS = (2, 6, 4)
LAYER_ORDER = [d ^ core for core in (0, 1) for d in (0,) + SECTION_STEPS]


def nt(a, b):
    return lax.dot_general(a, b, (((1,), (1,)), ((), ())), preferred_element_type=F32)


def tn(a, b):
    return lax.dot_general(a, b, (((0,), (0,)), ((), ())), preferred_element_type=F32)


def nn(a, b):
    return jnp.dot(a, b, preferred_element_type=F32)


def swap(value, axis, distance):
    count = lax.axis_size(axis)
    return lax.ppermute(value, axis, [(i, i ^ distance) for i in range(count)])


def turn(value, stage, step):
    sections, ways = lax.axis_size("section"), lax.axis_size("dp")
    pairs = []
    for s in range(sections):
        distance = RING[step] * (1 if s % 2 == stage else 4)
        pairs += [(s * ways + p, s * ways + (p ^ distance)) for p in range(ways)]
    return lax.ppermute(value, ("section", "dp"), pairs)


def iota(shape, dim):
    return lax.broadcasted_iota(jnp.int32, shape, dim)


def slot_of(codes, tok, cap):
    tokens = codes.shape[1]
    row, col = iota((tokens, tokens), 0), iota((tokens, tokens), 1)
    before = ((row < col) & (row // tok == col // tok)).astype(F32).astype(BF16)
    member = codes > 0.0
    rank = nn(member.astype(F32).astype(BF16), before).astype(jnp.int32)
    return jnp.where(member, rank + (iota(codes.shape, 1) // tok) * cap, -1)


def expert_signs(codes):
    experts = iota((codes.shape[0], 8, codes.shape[1]), 1).astype(F32)
    return (experts == 0.0).astype(F32) - (experts == codes[:, None, :]).astype(F32)


def diagonal(size):
    return (iota((size, size), 0) == iota((size, size), 1)).astype(F32)


def block_of(at, odd, way):
    apart = at ^ way
    low, high = apart & 3, apart >> 2
    low, high = low ^ (low >> 1), high ^ (high >> 1)
    return jnp.where(odd, 4 * low + high, 4 * high + low)


def left_block(rows, near, far, j, slots):
    turned = 4 * (j & 3) + (j >> 2)
    size = slots + 16
    members = rows[pl.ds(pl.multiple_of(j * size, 16), slots), :]
    routers = [near[17 * k + j] for k in range(4)] + [far[17 * k + turned] for k in range(4)]
    return jnp.concatenate([members] + routers, axis=0)


def layer_codes(near, far, tokens):
    return jnp.concatenate(
        [ref[17 * k + 16, 0:1, :tokens].astype(F32) for ref in (near, far) for k in range(4)],
        axis=0,
    )


def split(value):
    first = value.astype(BF16)
    rest = value - first.astype(F32)
    second = rest.astype(BF16)
    return [first, second, (rest - second.astype(F32)).astype(BF16)]


def pre_kernel(ins, raws, outs, raw_outs, *, cap):
    ids, grads, x, router = ins
    block, pick_out, code_out, mine_out = outs
    slots, tokens = pick_out.ref.shape
    tok = ids.ref.shape[1]
    micro = tokens // tok
    left = jnp.concatenate([ids.ref[2 * m:2 * m + 1, :] for m in range(micro)], axis=1)
    right = jnp.concatenate([ids.ref[2 * m + 1:2 * m + 2, :] for m in range(micro)], axis=1)
    code = jnp.where(left == 0, right, jnp.where(right == 0, left, 0)).astype(F32)
    code = jnp.broadcast_to(code, (16, tokens))
    code_out.ref[...] = jnp.zeros(code_out.ref.shape, BF16)
    code_out.ref[:, :tokens] = code.astype(BF16)
    code_out.flush()
    slot = slot_of(code[:8], tok, cap)[0:1]
    pick = (iota((slots, tokens), 0) == slot).astype(F32).astype(BF16)
    pick_out.ref[...] = pick
    pick_out.flush()
    block.ref[:slots, :] = nn(pick, grads.ref[...]).astype(BF16)
    me, _, _ = place()
    count = mine_out.ref.shape[0]
    own = count // micro
    wanted = iota((count, 1), 0)
    wanted = (wanted // own) * tok + me * own + wanted % own
    choose = (iota((count, tokens), 1) == wanted).astype(F32).astype(BF16)
    mine_out.ref[...] = nn(choose, grads.ref[...]).astype(BF16)
    mine_out.flush()
    logits = nt(router.ref[...], x.ref[...])
    apart = -jnp.sum(expert_signs(code[0:1])[0] * logits, axis=0, keepdims=True)
    parts = jnp.concatenate(split(apart) + [jnp.zeros((5, tokens), BF16)], axis=0)
    parts = jnp.concatenate(
        [nt(parts, pick), jnp.zeros((8, block.ref.shape[1] - slots), F32)], axis=1
    )
    both = jnp.concatenate([router.ref[...].astype(F32), parts], axis=0)
    block.ref[slots:, :] = both.astype(BF16)


def logit_parts(rows, slots, ways):
    apart = jnp.zeros((8, slots), F32)
    for j in range(ways):
        at = j * (slots + 16) + slots
        apart += rows[at:at + 16, :slots].astype(F32)[8:]
    return apart


def load_weights(w_ref, wbuf, sems, first):
    count = sems.shape[0]
    depth = wbuf.shape[0] // count
    copies = [
        pltpu.make_async_copy(
            w_ref.at[pl.ds(first + q * depth, depth)], wbuf.at[pl.ds(q * depth, depth)], sems.at[q]
        )
        for q in range(count)
    ]
    for copy in copies:
        copy.start()
    return copies


def load_rows(blocks, rows, sems):
    size = blocks[0].shape[0]
    loads = [
        pltpu.make_async_copy(block, rows.at[pl.ds(n * size, size)], sems.at[n])
        for n, block in enumerate(blocks)
    ]
    for load in loads:
        load.start()
    return loads


def back_kernel(ins, raws, outs, raw_outs, wbuf, sems, *, first):
    hid, back = ins[0], outs[0]
    copies = load_weights(raws[0], wbuf, sems, first)
    depth = wbuf.shape[0] // len(copies)
    hidden = hid.ref[...].T
    for q, copy in enumerate(copies):
        copy.wait()
        for part in range(4):
            rows = pl.ds(q * depth + part * (depth // 4), depth // 4)
            back.ref[rows, :] = nn(wbuf[rows, :], hidden).astype(BF16)


def mid_kernel(ins, raws, outs, raw_outs, rows, sems):
    pick, near, far, low, high = ins
    table_out, signs_out, gate_out = outs
    slots, width = pick.buffer.shape[0], near.buffer.shape[2]
    loads = load_rows(raws, rows, sems)
    me, at, odd = place()
    codes = layer_codes(near.ref, far.ref, pick.ref.shape[1])
    signs = expert_signs(nt(codes.astype(BF16), pick.ref[...]))
    layer = jnp.concatenate([jnp.full((1, 8, slots), d, jnp.int32) for d in LAYER_ORDER]) ^ me
    signs = jnp.where(layer > me, signs, 0.0)
    signs_out.ref[...] = signs
    filled = nt(jnp.ones((8, pick.buffer.shape[1]), BF16), pick.ref[...])
    for load in loads:
        load.wait()
    halves = (low.ref, high.ref)
    ways = 2 * (low.buffer.shape[0] // width)
    apart = jnp.sum(logit_parts(rows, slots, ways), axis=0, keepdims=True)
    gate = filled / (1.0 + jnp.exp(apart))
    gate_out.ref[...] = gate
    slope = gate * (1.0 - gate)
    total = jnp.zeros((slots + signs.shape[0] * 8, slots), F32)
    for way in range(0, ways, 2):
        left = jnp.concatenate([
            left_block(rows, near.ref, far.ref, block_of(at, odd, way + i), slots)
            for i in range(2)
        ], axis=1)
        at_row = way % (ways // 2) * width
        total += nn(left, halves[way * 2 // ways][at_row:at_row + 2 * width])
    base = jnp.sum(diagonal(slots) * total[:slots], axis=0, keepdims=True)
    coefs = jnp.sum(signs * total[slots:].reshape(signs.shape), axis=1)
    table = jnp.where(iota(coefs.shape, 0) == 0, base, coefs) * slope
    table = jnp.concatenate([table.astype(BF16)] * 2, axis=0)
    table_out.ref[...] = jnp.broadcast_to(table[None], table_out.ref.shape)
    table_out.flush()


def side_kernel(ins, raws, outs, raw_outs, rows, lsems, wbuf, sems, *, tok, cap):
    near, far, hid, gate = ins
    picks_out, scaled_out, codes_out, product_out, mixed_out = outs
    slots, width = hid.buffer.shape[0], near.buffer.shape[2]
    loads = load_rows(raws[:4], rows, lsems)
    copies = load_weights(raws[4], wbuf, sems, 0)
    me, at, odd = place()
    codes = layer_codes(near.ref, far.ref, codes_out.ref.shape[1])
    codes_out.ref[...] = codes
    codes_out.flush()
    slot = slot_of(codes, tok, cap)
    for i, d in enumerate(LAYER_ORDER):
        pick = (iota((slots, slot.shape[1]), 0) == slot[i:i + 1]).astype(F32).astype(BF16)
        picks_out.ref[me ^ d] = pick
    picks_out.flush()
    gate_col = jnp.sum(diagonal(slots) * gate.ref[0:1], axis=1, keepdims=True)
    scaled_out.ref[...] = (gate_col * hid.ref[...].astype(F32)).astype(BF16)
    scaled_out.flush()
    for load in loads:
        load.wait()
    ways = wbuf.shape[0] // width
    total = jnp.zeros((slots + mixed_out.ref.shape[0], mixed_out.ref.shape[1]), F32)
    for way in range(0, ways, 2):
        left = jnp.concatenate([
            left_block(rows, near.ref, far.ref, block_of(at, odd, way + i), slots)
            for i in range(2)
        ], axis=1)
        if way * len(copies) % ways == 0:
            copies[way * len(copies) // ways].wait()
        total += nn(left, wbuf[way * width:(way + 2) * width])
    product_out.ref[...] = total[:slots]
    mixed_out.ref[...] = total[slots:].astype(BF16)


def tail_kernel(ins, raws, outs, raw_outs, delta_ref, step_ref, rows, lsems, obuf, sems):
    got, picks, codes, signs, pick, scaled_in, near, far, product, mixed, gate, x, grads = ins
    blocks, down_ref = raws, raw_outs[0]
    input_out, hidden_out, router_out = outs
    layers, slots = codes.buffer.shape[0], gate.buffer.shape[1]
    tokens, width = codes.buffer.shape[1], x.buffer.shape[1]
    ways = obuf.shape[0] // width
    loads = load_rows(blocks, rows, lsems)
    me, at, odd = place()
    parts_of = []
    for s in range(layers):
        table = got.ref[s]
        parts = nn(jnp.concatenate(split(table), axis=0), picks.ref[s])
        parts_of.append(parts[:8] + parts[8:16] + parts[16:])
    deltas = [None] * layers
    for layer in range(layers - 1, -1, -1):
        value = parts_of[layer][0:1]
        for upper in range(layer + 1, layers):
            i = LAYER_ORDER.index(layer ^ upper)
            value += deltas[upper] * parts_of[layer][i:i + 1]
        deltas[layer] = value.astype(BF16).astype(F32)
        delta_ref[layer:layer + 1, :] = deltas[layer]
    mine = jnp.concatenate([delta_ref[pl.ds(me ^ d, 1), :] for d in LAYER_ORDER], axis=0)
    delta_slot = nt(mine.astype(BF16), pick.ref[...])
    lift = (signs.ref[...] * delta_slot[:, None, :]).reshape(layers * 8, slots).astype(BF16)
    scaled = scaled_in.ref[...]
    right = jnp.concatenate([scaled, nn(lift, scaled).astype(BF16)], axis=0)
    for load in loads:
        load.wait()
    copies = []
    for way in range(ways):
        left = left_block(rows, near.ref, far.ref, block_of(at, odd, way), slots)
        obuf[way * width:(way + 1) * width] = tn(left, right).astype(BF16)
        if way % 2 == 1:
            done = pl.ds((way - 1) * width, 2 * width)
            copies.append(
                pltpu.make_async_copy(obuf.at[done], down_ref.at[done], sems.at[way // 2])
            )
            copies[-1].start()
    gate_col = jnp.sum(diagonal(slots) * gate.ref[0:1], axis=1, keepdims=True)
    hidden = product.ref[...] + tn(lift, mixed.ref[...])
    hidden_out.ref[...] = (gate_col * hidden).astype(BF16)
    hidden_out.flush()
    logit_grads = expert_signs(codes.ref[...]) * mine[:, None, :]
    router_out.ref[...] = nn(logit_grads[0].astype(BF16), x.ref[...])
    router_out.flush()
    local = jnp.concatenate([ref[17 * k] for ref in (near.ref, far.ref) for k in range(4)], axis=0)
    step_ref[...] = tn(logit_grads.reshape(layers * 8, tokens).astype(BF16), local)
    count = 4
    own, tok = grads.buffer.shape[0] // count, tokens // count
    steps = jnp.concatenate([
        step_ref[pl.ds(pl.multiple_of(m * tok + me * own, 8), own), :] for m in range(count)
    ], axis=0)
    input_out.ref[...] = (grads.ref[...].astype(F32) + steps).astype(BF16)
    input_out.flush()
    for copy in copies:
        copy.wait()


class Staged:
    def __init__(self, source, buffer, semaphore):
        self.copy = pltpu.make_async_copy(source, buffer, semaphore)
        self.copy.start()
        self.buffer, self.waited = buffer, False

    @property
    def ref(self):
        if not self.waited:
            self.copy.wait()
            self.waited = True
        return self.buffer


class Result:
    def __init__(self, buffer, target, semaphore):
        self.ref, self.copy, self.sent = buffer, None, False
        self.parts = (buffer, target, semaphore)

    def flush(self):
        if not self.sent:
            self.copy = pltpu.make_async_copy(*self.parts)
            self.copy.start()
            self.sent = True


def call(kernel, staged, raw, results, raw_results=(), scratch=(), flops=0, moved=0):
    counts = (len(staged), len(raw), len(results), len(raw_results))

    def body(*refs):
        groups, at = [], 0
        for count in counts + (counts[0], counts[2]):
            groups.append(refs[at:at + count])
            at += count
        sources, raws, targets, raw_targets, ibufs, obufs = groups
        sems, rest = refs[at], refs[at + 1:]
        ins = [Staged(r, v, sems.at[n]) for n, (r, v) in enumerate(zip(sources, ibufs))]
        outs = [
            Result(v, r, sems.at[counts[0] + n]) for n, (r, v) in enumerate(zip(targets, obufs))
        ]
        kernel(ins, raws, outs, raw_targets, *rest)
        for item in ins:
            item.ref
        for item in outs:
            item.flush()
        for item in outs:
            item.copy.wait()

    shapes = [jax.ShapeDtypeStruct(*o) for o in results] + [
        jax.ShapeDtypeStruct(*o) for o in raw_results
    ]
    return pl.pallas_call(
        body,
        out_shape=shapes,
        in_specs=[HBM] * (counts[0] + counts[1]),
        out_specs=[HBM] * len(shapes),
        scratch_shapes=[pltpu.VMEM(v.shape, v.dtype) for v in staged]
        + [pltpu.VMEM(*o) for o in results]
        + [pltpu.SemaphoreType.DMA((counts[0] + counts[2],))]
        + list(scratch),
        compiler_params=pltpu.CompilerParams(vmem_limit_bytes=GRANT),
        cost_estimate=pl.CostEstimate(flops=flops, bytes_accessed=moved, transcendentals=0),
    )(*staged, *raw)


def place():
    me, at = lax.axis_index("section"), lax.axis_index("dp")
    return me, at, (me & 1) == 1


def per_device(layer_inputs, expert_ids, hidden, down_weight, router_weight, grad_out):
    sections, ways = lax.axis_size("section"), lax.axis_size("dp")
    micro, tok, width = grad_out.shape
    cap, units = hidden.shape[2:]
    experts = router_weight.shape[2]
    tokens, slots = micro * tok, micro * cap
    full = ways * width
    x = layer_inputs[0].reshape(tokens, width)
    hid = hidden[0].reshape(slots, units)
    router = router_weight[0].T
    grads = grad_out.reshape(tokens, width)

    own = tok // sections
    block, pick, code, grads_mine = call(
        lambda *refs: pre_kernel(*refs, cap=cap),
        [expert_ids[0].transpose(0, 2, 1).reshape(2 * micro, tok), grads, x, router],
        [],
        [((slots + 16, width), BF16), ((slots, tokens), BF16), ((16, width), BF16),
         ((micro * own, width), BF16)],
    )

    weights = down_weight[0]

    def back(after, first):
        after, hid_after = lax.optimization_barrier((after, hid))
        return after, call(
            lambda *refs: back_kernel(*refs, first=first),
            [hid_after],
            [weights],
            [((full // 2, slots), BF16)],
            scratch=[pltpu.VMEM((full // 2, units), BF16), pltpu.SemaphoreType.DMA((2,))],
            moved=full * units,
        )[0]

    block, low = back(block, 0)
    group = [block] + [turn(block, 0, step) for step in (1, 2, 3)]
    group, low = lax.optimization_barrier((group, low))
    group = jnp.stack(group)
    routers, high = back(group[:, slots:slots + experts], full // 2)
    routers = [routers] + [turn(routers, 1, step) for step in (1, 2, 3)]
    routers, high = lax.optimization_barrier((routers, high))
    blocks = [group] + [turn(group, 1, step) for step in (1, 2, 3)]
    blocks = [b.reshape(4 * (slots + 16), width) for b in blocks]
    mine = jnp.concatenate(routers + [code[None, :experts]])
    near = jnp.concatenate([mine] + [swap(mine, "section", d) for d in SECTION_STEPS])
    far = swap(near, "section", 1)

    rows_buffer = pltpu.VMEM((ways * (slots + 16), width), BF16)
    table, signs, gate = call(
        mid_kernel,
        [pick, near, far, low, high],
        blocks,
        [
            ((sections * ways // 2, 2 * sections, slots), BF16),
            ((sections, experts, slots), F32),
            ((8, slots), F32),
        ],
        scratch=[rows_buffer, pltpu.SemaphoreType.DMA((4,))],
    )
    table = table.reshape(sections * ways, sections, slots)
    got_table = lax.all_to_all(table, ("section", "dp"), 0, 0, tiled=True)

    table_sum = jnp.sum(
        got_table.reshape(sections, ways, sections, slots).astype(F32), axis=1
    )
    picks, scaled, codes, product, mixed = call(
        lambda *refs: side_kernel(*refs, tok=tok, cap=cap),
        [near, far, hid, gate],
        blocks + [weights],
        [
            ((sections, slots, tokens), BF16),
            ((slots, units), BF16),
            ((sections, tokens), F32),
            ((slots, units), F32),
            ((sections * experts, units), BF16),
        ],
        scratch=[
            rows_buffer,
            pltpu.SemaphoreType.DMA((4,)),
            pltpu.VMEM((full, units), BF16),
            pltpu.SemaphoreType.DMA((4,)),
        ],
        flops=10**9,
        moved=10**7,
    )
    input_grad, hidden_grad, router_grad, down_grad = call(
        tail_kernel,
        [
            table_sum, picks, codes, signs, pick, scaled, near, far,
            product, mixed, gate, x, grads_mine,
        ],
        blocks,
        [
            ((micro * own, width), BF16),
            ((slots, units), BF16),
            ((experts, width), F32),
        ],
        raw_results=[((full, units), BF16)],
        scratch=[
            pltpu.VMEM((sections, tokens), F32),
            pltpu.VMEM((tokens, width), F32),
            rows_buffer,
            pltpu.SemaphoreType.DMA((4,)),
            pltpu.VMEM((full, units), BF16),
            pltpu.SemaphoreType.DMA((ways // 2,)),
        ],
        flops=2 * 192 * full * units,
        moved=full * units * 2,
    )
    return (
        input_grad.reshape(micro, own, width),
        hidden_grad.reshape(1, micro, cap, units),
        down_grad[None],
        router_grad.T[None],
    )


def solution(mesh):
    return jax.shard_map(
        per_device,
        mesh=mesh,
        in_specs=(
            P("section", None, None, "dp"),
            P("section", None, None, None),
            P("section", None, None, "dp"),
            P("section", None, "dp"),
            P("section", "dp", None),
            P(None, None, "dp"),
        ),
        out_specs=(
            P(None, "section", "dp"),
            P("section", None, None, "dp"),
            P("section", None, "dp"),
            P("section", "dp", None),
        ),
        check_vma=False,
    )
```

```python
import jax
import jax.numpy as jnp
from jax import lax
from jax.experimental import pallas as pl
from jax.experimental.pallas import tpu as pltpu
from jax.sharding import PartitionSpec as P

F32 = jnp.float32
BF16 = jnp.bfloat16
HBM = pl.BlockSpec(memory_space=pltpu.HBM)
GRANT = 62 << 20
RING = (0, 1, 3, 2)
SECTION_STEPS = (2, 6, 4)
LAYER_ORDER = [d ^ core for core in (0, 1) for d in (0,) + SECTION_STEPS]


def nt(a, b):
    return lax.dot_general(a, b, (((1,), (1,)), ((), ())), preferred_element_type=F32)


def tn(a, b):
    return lax.dot_general(a, b, (((0,), (0,)), ((), ())), preferred_element_type=F32)


def nn(a, b):
    return jnp.dot(a, b, preferred_element_type=F32)


def swap(value, axis, distance):
    count = lax.axis_size(axis)
    return lax.ppermute(value, axis, [(i, i ^ distance) for i in range(count)])


def turn(value, stage, step):
    sections, ways = lax.axis_size("section"), lax.axis_size("dp")
    pairs = []
    for s in range(sections):
        distance = RING[step] * (1 if s % 2 == stage else 4)
        pairs += [(s * ways + p, s * ways + (p ^ distance)) for p in range(ways)]
    return lax.ppermute(value, ("section", "dp"), pairs)


def iota(shape, dim):
    return lax.broadcasted_iota(jnp.int32, shape, dim)


def slot_of(codes, tok, cap):
    tokens = codes.shape[1]
    row, col = iota((tokens, tokens), 0), iota((tokens, tokens), 1)
    before = ((row < col) & (row // tok == col // tok)).astype(F32).astype(BF16)
    member = codes > 0.0
    rank = nn(member.astype(F32).astype(BF16), before).astype(jnp.int32)
    return jnp.where(member, rank + (iota(codes.shape, 1) // tok) * cap, -1)


def expert_signs(codes):
    experts = iota((codes.shape[0], 8, codes.shape[1]), 1).astype(F32)
    return (experts == 0.0).astype(F32) - (experts == codes[:, None, :]).astype(F32)


def diagonal(size):
    return (iota((size, size), 0) == iota((size, size), 1)).astype(F32)


def block_of(at, odd, way):
    apart = at ^ way
    low, high = apart & 3, apart >> 2
    low, high = low ^ (low >> 1), high ^ (high >> 1)
    return jnp.where(odd, 4 * low + high, 4 * high + low)


def left_block(rows, near, far, j, slots):
    turned = 4 * (j & 3) + (j >> 2)
    size = slots + 16
    members = rows[pl.ds(pl.multiple_of(j * size, 16), slots), :]
    routers = [near[17 * k + j] for k in range(4)] + [far[17 * k + turned] for k in range(4)]
    return jnp.concatenate([members] + routers, axis=0)


def layer_codes(near, far, tokens):
    return jnp.concatenate(
        [ref[17 * k + 16, 0:1, :tokens].astype(F32) for ref in (near, far) for k in range(4)],
        axis=0,
    )


def split(value):
    first = value.astype(BF16)
    rest = value - first.astype(F32)
    second = rest.astype(BF16)
    return [first, second, (rest - second.astype(F32)).astype(BF16)]


def pre_kernel(ins, raws, outs, raw_outs, *, cap):
    ids, grads, x, router = ins
    block, pick_out, code_out = outs
    slots, tokens = pick_out.ref.shape
    tok = ids.ref.shape[1]
    micro = tokens // tok
    left = jnp.concatenate([ids.ref[2 * m:2 * m + 1, :] for m in range(micro)], axis=1)
    right = jnp.concatenate([ids.ref[2 * m + 1:2 * m + 2, :] for m in range(micro)], axis=1)
    code = jnp.where(left == 0, right, jnp.where(right == 0, left, 0)).astype(F32)
    code = jnp.broadcast_to(code, (16, tokens))
    code_out.ref[...] = jnp.zeros(code_out.ref.shape, BF16)
    code_out.ref[:, :tokens] = code.astype(BF16)
    code_out.flush()
    slot = slot_of(code[:8], tok, cap)[0:1]
    pick = (iota((slots, tokens), 0) == slot).astype(F32).astype(BF16)
    pick_out.ref[...] = pick
    pick_out.flush()
    block.ref[:slots, :] = nn(pick, grads.ref[...]).astype(BF16)
    logits = nt(router.ref[...], x.ref[...])
    apart = -jnp.sum(expert_signs(code[0:1])[0] * logits, axis=0, keepdims=True)
    parts = jnp.concatenate(split(apart) + [jnp.zeros((5, tokens), BF16)], axis=0)
    parts = jnp.concatenate(
        [nt(parts, pick), jnp.zeros((8, block.ref.shape[1] - slots), F32)], axis=1
    )
    both = jnp.concatenate([router.ref[...].astype(F32), parts], axis=0)
    block.ref[slots:, :] = both.astype(BF16)


def logit_parts(rows, slots, ways):
    apart = jnp.zeros((8, slots), F32)
    for j in range(ways):
        at = j * (slots + 16) + slots
        apart += rows[at:at + 16, :slots].astype(F32)[8:]
    return apart


def load_weights(w_ref, wbuf, sems, first):
    count = sems.shape[0]
    depth = wbuf.shape[0] // count
    copies = [
        pltpu.make_async_copy(
            w_ref.at[pl.ds(first + q * depth, depth)], wbuf.at[pl.ds(q * depth, depth)], sems.at[q]
        )
        for q in range(count)
    ]
    for copy in copies:
        copy.start()
    return copies


def load_rows(blocks, rows, sems):
    size = blocks[0].shape[0]
    loads = [
        pltpu.make_async_copy(block, rows.at[pl.ds(n * size, size)], sems.at[n])
        for n, block in enumerate(blocks)
    ]
    for load in loads:
        load.start()
    return loads


def back_kernel(ins, raws, outs, raw_outs, wbuf, sems, *, first):
    hid, back = ins[0], outs[0]
    copies = load_weights(raws[0], wbuf, sems, first)
    depth = wbuf.shape[0] // len(copies)
    hidden = hid.ref[...].T
    for q, copy in enumerate(copies):
        copy.wait()
        for part in range(4):
            rows = pl.ds(q * depth + part * (depth // 4), depth // 4)
            back.ref[rows, :] = nn(wbuf[rows, :], hidden).astype(BF16)


def mid_kernel(ins, raws, outs, raw_outs, rows, sems):
    pick, near, far, low, high = ins
    table_out, signs_out, gate_out = outs
    slots, width = pick.buffer.shape[0], near.buffer.shape[2]
    loads = load_rows(raws, rows, sems)
    me, at, odd = place()
    codes = layer_codes(near.ref, far.ref, pick.ref.shape[1])
    signs = expert_signs(nt(codes.astype(BF16), pick.ref[...]))
    layer = jnp.concatenate([jnp.full((1, 8, slots), d, jnp.int32) for d in LAYER_ORDER]) ^ me
    signs = jnp.where(layer > me, signs, 0.0)
    signs_out.ref[...] = signs
    signs_out.flush()
    filled = nt(jnp.ones((8, pick.buffer.shape[1]), BF16), pick.ref[...])
    for load in loads:
        load.wait()
    halves = (low.ref, high.ref)
    ways = 2 * (low.buffer.shape[0] // width)
    apart = jnp.sum(logit_parts(rows, slots, ways), axis=0, keepdims=True)
    gate = filled / (1.0 + jnp.exp(apart))
    gate_out.ref[...] = gate
    gate_out.flush()
    slope = gate * (1.0 - gate)
    total = jnp.zeros((slots + signs.shape[0] * 8, slots), F32)
    for way in range(0, ways, 2):
        left = jnp.concatenate([
            left_block(rows, near.ref, far.ref, block_of(at, odd, way + i), slots)
            for i in range(2)
        ], axis=1)
        at_row = way % (ways // 2) * width
        total += nn(left, halves[way * 2 // ways][at_row:at_row + 2 * width])
    base = jnp.sum(diagonal(slots) * total[:slots], axis=0, keepdims=True)
    coefs = jnp.sum(signs * total[slots:].reshape(signs.shape), axis=1)
    table = jnp.where(iota(coefs.shape, 0) == 0, base, coefs) * slope
    table = jnp.concatenate([table.astype(BF16)] * 2, axis=0)
    table_out.ref[...] = jnp.broadcast_to(table[None], table_out.ref.shape)
    table_out.flush()


def side_kernel(ins, raws, outs, raw_outs, rows, lsems, wbuf, sems, *, tok, cap):
    near, far, hid, gate, grads = ins
    picks_out, scaled_out, codes_out, mine_out, product_out, mixed_out = outs
    slots, width = hid.buffer.shape[0], near.buffer.shape[2]
    loads = load_rows(raws[:4], rows, lsems)
    copies = load_weights(raws[4], wbuf, sems, 0)
    me, at, odd = place()
    codes = layer_codes(near.ref, far.ref, codes_out.ref.shape[1])
    codes_out.ref[...] = codes
    codes_out.flush()
    slot = slot_of(codes, tok, cap)
    for i, d in enumerate(LAYER_ORDER):
        pick = (iota((slots, slot.shape[1]), 0) == slot[i:i + 1]).astype(F32).astype(BF16)
        picks_out.ref[me ^ d] = pick
    picks_out.flush()
    gate_col = jnp.sum(diagonal(slots) * gate.ref[0:1], axis=1, keepdims=True)
    scaled_out.ref[...] = (gate_col * hid.ref[...].astype(F32)).astype(BF16)
    scaled_out.flush()
    count, tokens = mine_out.ref.shape[0], grads.buffer.shape[0]
    own = count * tok // tokens
    wanted = iota((count, 1), 0)
    wanted = (wanted // own) * tok + me * own + wanted % own
    choose = (iota((count, tokens), 1) == wanted).astype(F32).astype(BF16)
    mine_out.ref[...] = nn(choose, grads.ref[...]).astype(BF16)
    mine_out.flush()
    for load in loads:
        load.wait()
    ways = wbuf.shape[0] // width
    total = jnp.zeros((slots + mixed_out.ref.shape[0], mixed_out.ref.shape[1]), F32)
    for way in range(0, ways, 2):
        left = jnp.concatenate([
            left_block(rows, near.ref, far.ref, block_of(at, odd, way + i), slots)
            for i in range(2)
        ], axis=1)
        if way * len(copies) % ways == 0:
            copies[way * len(copies) // ways].wait()
        total += nn(left, wbuf[way * width:(way + 2) * width])
    product_out.ref[...] = total[:slots]
    mixed_out.ref[...] = total[slots:].astype(BF16)


def tail_kernel(ins, raws, outs, raw_outs, delta_ref, step_ref, rows, lsems, obuf, sems):
    got, picks, codes, signs, pick, scaled_in, near, far, product, mixed, gate, x, grads = ins
    blocks, down_ref = raws, raw_outs[0]
    input_out, hidden_out, router_out = outs
    layers, slots = codes.buffer.shape[0], gate.buffer.shape[1]
    tokens, width = codes.buffer.shape[1], x.buffer.shape[1]
    ways = obuf.shape[0] // width
    loads = load_rows(blocks, rows, lsems)
    me, at, odd = place()
    parts_of = []
    for s in range(layers):
        table = got.ref[s]
        parts = nn(jnp.concatenate(split(table), axis=0), picks.ref[s])
        parts_of.append(parts[:8] + parts[8:16] + parts[16:])
    deltas = [None] * layers
    for layer in range(layers - 1, -1, -1):
        value = parts_of[layer][0:1]
        for upper in range(layer + 1, layers):
            i = LAYER_ORDER.index(layer ^ upper)
            value += deltas[upper] * parts_of[layer][i:i + 1]
        deltas[layer] = value.astype(BF16).astype(F32)
        delta_ref[layer:layer + 1, :] = deltas[layer]
    mine = jnp.concatenate([delta_ref[pl.ds(me ^ d, 1), :] for d in LAYER_ORDER], axis=0)
    delta_slot = nt(mine.astype(BF16), pick.ref[...])
    lift = (signs.ref[...] * delta_slot[:, None, :]).reshape(layers * 8, slots).astype(BF16)
    scaled = scaled_in.ref[...]
    right = jnp.concatenate([scaled, nn(lift, scaled).astype(BF16)], axis=0)
    for load in loads:
        load.wait()
    copies = []
    for way in range(ways):
        left = left_block(rows, near.ref, far.ref, block_of(at, odd, way), slots)
        obuf[way * width:(way + 1) * width] = tn(left, right).astype(BF16)
        if way % 2 == 1:
            done = pl.ds((way - 1) * width, 2 * width)
            copies.append(
                pltpu.make_async_copy(obuf.at[done], down_ref.at[done], sems.at[way // 2])
            )
            copies[-1].start()
    gate_col = jnp.sum(diagonal(slots) * gate.ref[0:1], axis=1, keepdims=True)
    hidden = product.ref[...] + tn(lift, mixed.ref[...])
    hidden_out.ref[...] = (gate_col * hidden).astype(BF16)
    hidden_out.flush()
    logit_grads = expert_signs(codes.ref[...]) * mine[:, None, :]
    router_out.ref[...] = nn(logit_grads[0].astype(BF16), x.ref[...])
    router_out.flush()
    local = jnp.concatenate([ref[17 * k] for ref in (near.ref, far.ref) for k in range(4)], axis=0)
    step_ref[...] = tn(logit_grads.reshape(layers * 8, tokens).astype(BF16), local)
    count = 4
    own, tok = grads.buffer.shape[0] // count, tokens // count
    steps = jnp.concatenate([
        step_ref[pl.ds(pl.multiple_of(m * tok + me * own, 8), own), :] for m in range(count)
    ], axis=0)
    input_out.ref[...] = (grads.ref[...].astype(F32) + steps).astype(BF16)
    input_out.flush()
    for copy in copies:
        copy.wait()


class Staged:
    def __init__(self, source, buffer, semaphore):
        self.copy = pltpu.make_async_copy(source, buffer, semaphore)
        self.copy.start()
        self.buffer, self.waited = buffer, False

    @property
    def ref(self):
        if not self.waited:
            self.copy.wait()
            self.waited = True
        return self.buffer


class Result:
    def __init__(self, buffer, target, semaphore):
        self.ref, self.copy, self.sent = buffer, None, False
        self.parts = (buffer, target, semaphore)

    def flush(self):
        if not self.sent:
            self.copy = pltpu.make_async_copy(*self.parts)
            self.copy.start()
            self.sent = True


def call(kernel, staged, raw, results, raw_results=(), scratch=(), flops=0, moved=0):
    counts = (len(staged), len(raw), len(results), len(raw_results))

    def body(*refs):
        groups, at = [], 0
        for count in counts + (counts[0], counts[2]):
            groups.append(refs[at:at + count])
            at += count
        sources, raws, targets, raw_targets, ibufs, obufs = groups
        sems, rest = refs[at], refs[at + 1:]
        ins = [Staged(r, v, sems.at[n]) for n, (r, v) in enumerate(zip(sources, ibufs))]
        outs = [
            Result(v, r, sems.at[counts[0] + n]) for n, (r, v) in enumerate(zip(targets, obufs))
        ]
        kernel(ins, raws, outs, raw_targets, *rest)
        for item in ins:
            item.ref
        for item in outs:
            item.flush()
        for item in outs:
            item.copy.wait()

    shapes = [jax.ShapeDtypeStruct(*o) for o in results] + [
        jax.ShapeDtypeStruct(*o) for o in raw_results
    ]
    return pl.pallas_call(
        body,
        out_shape=shapes,
        in_specs=[HBM] * (counts[0] + counts[1]),
        out_specs=[HBM] * len(shapes),
        scratch_shapes=[pltpu.VMEM(v.shape, v.dtype) for v in staged]
        + [pltpu.VMEM(*o) for o in results]
        + [pltpu.SemaphoreType.DMA((counts[0] + counts[2],))]
        + list(scratch),
        compiler_params=pltpu.CompilerParams(vmem_limit_bytes=GRANT),
        cost_estimate=pl.CostEstimate(flops=flops, bytes_accessed=moved, transcendentals=0),
    )(*staged, *raw)


def place():
    me, at = lax.axis_index("section"), lax.axis_index("dp")
    return me, at, (me & 1) == 1


def per_device(layer_inputs, expert_ids, hidden, down_weight, router_weight, grad_out):
    sections, ways = lax.axis_size("section"), lax.axis_size("dp")
    micro, tok, width = grad_out.shape
    cap, units = hidden.shape[2:]
    experts = router_weight.shape[2]
    tokens, slots = micro * tok, micro * cap
    full = ways * width
    x = layer_inputs[0].reshape(tokens, width)
    hid = hidden[0].reshape(slots, units)
    router = router_weight[0].T
    grads = grad_out.reshape(tokens, width)

    own = tok // sections
    block, pick, code = call(
        lambda *refs: pre_kernel(*refs, cap=cap),
        [expert_ids[0].transpose(0, 2, 1).reshape(2 * micro, tok), grads, x, router],
        [],
        [((slots + 16, width), BF16), ((slots, tokens), BF16), ((16, width), BF16)],
    )

    weights = down_weight[0]

    def back(after, first):
        after, hid_after = lax.optimization_barrier((after, hid))
        return after, call(
            lambda *refs: back_kernel(*refs, first=first),
            [hid_after],
            [weights],
            [((full // 2, slots), BF16)],
            scratch=[pltpu.VMEM((full // 2, units), BF16), pltpu.SemaphoreType.DMA((2,))],
            moved=full * units,
        )[0]

    block, low = back(block, 0)
    group = [block] + [turn(block, 0, step) for step in (1, 2, 3)]
    group, low = lax.optimization_barrier((group, low))
    group = jnp.stack(group)
    routers, high = back(group[:, slots:slots + experts], full // 2)
    routers = [routers] + [turn(routers, 1, step) for step in (1, 2, 3)]
    routers, high = lax.optimization_barrier((routers, high))
    blocks = [group] + [turn(group, 1, step) for step in (1, 2, 3)]
    blocks = [b.reshape(4 * (slots + 16), width) for b in blocks]
    mine = jnp.concatenate(routers + [code[None, :experts]])
    near = jnp.concatenate([mine] + [swap(mine, "section", d) for d in SECTION_STEPS])
    far = swap(near, "section", 1)

    rows_buffer = pltpu.VMEM((ways * (slots + 16), width), BF16)
    table, signs, gate = call(
        mid_kernel,
        [pick, near, far, low, high],
        blocks,
        [
            ((sections * ways // 2, 2 * sections, slots), BF16),
            ((sections, experts, slots), F32),
            ((8, slots), F32),
        ],
        scratch=[rows_buffer, pltpu.SemaphoreType.DMA((4,))],
    )
    table = table.reshape(sections * ways, sections, slots)
    got_table = lax.all_to_all(table, ("section", "dp"), 0, 0, tiled=True)

    table_sum = jnp.sum(
        got_table.reshape(sections, ways, sections, slots).astype(F32), axis=1
    )
    picks, scaled, codes, grads_mine, product, mixed = call(
        lambda *refs: side_kernel(*refs, tok=tok, cap=cap),
        [near, far, hid, gate, grads],
        blocks + [weights],
        [
            ((sections, slots, tokens), BF16),
            ((slots, units), BF16),
            ((sections, tokens), F32),
            ((micro * own, width), BF16),
            ((slots, units), F32),
            ((sections * experts, units), BF16),
        ],
        scratch=[
            rows_buffer,
            pltpu.SemaphoreType.DMA((4,)),
            pltpu.VMEM((full, units), BF16),
            pltpu.SemaphoreType.DMA((4,)),
        ],
        flops=10**9,
        moved=10**7,
    )
    input_grad, hidden_grad, router_grad, down_grad = call(
        tail_kernel,
        [
            table_sum, picks, codes, signs, pick, scaled, near, far,
            product, mixed, gate, x, grads_mine,
        ],
        blocks,
        [
            ((micro * own, width), BF16),
            ((slots, units), BF16),
            ((experts, width), F32),
        ],
        raw_results=[((full, units), BF16)],
        scratch=[
            pltpu.VMEM((sections, tokens), F32),
            pltpu.VMEM((tokens, width), F32),
            rows_buffer,
            pltpu.SemaphoreType.DMA((4,)),
            pltpu.VMEM((full, units), BF16),
            pltpu.SemaphoreType.DMA((ways // 2,)),
        ],
        flops=2 * 192 * full * units,
        moved=full * units * 2,
    )
    return (
        input_grad.reshape(micro, own, width),
        hidden_grad.reshape(1, micro, cap, units),
        down_grad[None],
        router_grad.T[None],
    )


def solution(mesh):
    return jax.shard_map(
        per_device,
        mesh=mesh,
        in_specs=(
            P("section", None, None, "dp"),
            P("section", None, None, None),
            P("section", None, None, "dp"),
            P("section", None, "dp"),
            P("section", "dp", None),
            P(None, None, "dp"),
        ),
        out_specs=(
            P(None, "section", "dp"),
            P("section", None, None, "dp"),
            P("section", None, "dp"),
            P("section", "dp", None),
        ),
        check_vma=False,
    )
```

```python
import jax
import jax.numpy as jnp
from jax import lax
from jax.experimental import pallas as pl
from jax.experimental.pallas import tpu as pltpu
from jax.sharding import PartitionSpec as P

F32 = jnp.float32
BF16 = jnp.bfloat16
HBM = pl.BlockSpec(memory_space=pltpu.HBM)
GRANT = 62 << 20
RING = (0, 1, 3, 2)
SECTION_STEPS = (2, 6, 4)
LAYER_ORDER = [d ^ core for core in (0, 1) for d in (0,) + SECTION_STEPS]


def nt(a, b):
    return lax.dot_general(a, b, (((1,), (1,)), ((), ())), preferred_element_type=F32)


def tn(a, b):
    return lax.dot_general(a, b, (((0,), (0,)), ((), ())), preferred_element_type=F32)


def nn(a, b):
    return jnp.dot(a, b, preferred_element_type=F32)


def swap(value, axis, distance):
    count = lax.axis_size(axis)
    return lax.ppermute(value, axis, [(i, i ^ distance) for i in range(count)])


def turn(value, stage, step):
    sections, ways = lax.axis_size("section"), lax.axis_size("dp")
    pairs = []
    for s in range(sections):
        distance = RING[step] * (1 if s % 2 == stage else 4)
        pairs += [(s * ways + p, s * ways + (p ^ distance)) for p in range(ways)]
    return lax.ppermute(value, ("section", "dp"), pairs)


def iota(shape, dim):
    return lax.broadcasted_iota(jnp.int32, shape, dim)


def slot_of(codes, tok, cap):
    tokens = codes.shape[1]
    row, col = iota((tokens, tokens), 0), iota((tokens, tokens), 1)
    before = ((row < col) & (row // tok == col // tok)).astype(F32).astype(BF16)
    member = codes > 0.0
    rank = nn(member.astype(F32).astype(BF16), before).astype(jnp.int32)
    return jnp.where(member, rank + (iota(codes.shape, 1) // tok) * cap, -1)


def expert_signs(codes):
    experts = iota((codes.shape[0], 8, codes.shape[1]), 1).astype(F32)
    return (experts == 0.0).astype(F32) - (experts == codes[:, None, :]).astype(F32)


def diagonal(size):
    return (iota((size, size), 0) == iota((size, size), 1)).astype(F32)


def block_of(at, odd, way):
    apart = at ^ way
    low, high = apart & 3, apart >> 2
    low, high = low ^ (low >> 1), high ^ (high >> 1)
    return jnp.where(odd, 4 * low + high, 4 * high + low)


def left_block(rows, near, far, j, slots):
    turned = 4 * (j & 3) + (j >> 2)
    size = slots + 16
    members = rows[pl.ds(pl.multiple_of(j * size, 16), slots), :]
    routers = [near[17 * k + j] for k in range(4)] + [far[17 * k + turned] for k in range(4)]
    return jnp.concatenate([members] + routers, axis=0)


def layer_codes(near, far, tokens):
    return jnp.concatenate(
        [ref[17 * k + 16, 0:1, :tokens].astype(F32) for ref in (near, far) for k in range(4)],
        axis=0,
    )


def split(value):
    first = value.astype(BF16)
    rest = value - first.astype(F32)
    second = rest.astype(BF16)
    return [first, second, (rest - second.astype(F32)).astype(BF16)]


def pre_kernel(ins, raws, outs, raw_outs, *, cap):
    ids, grads, x, router = ins
    block, pick_out, code_out, mine_out = outs
    slots, tokens = pick_out.ref.shape
    tok = ids.ref.shape[1]
    micro = tokens // tok
    left = jnp.concatenate([ids.ref[2 * m:2 * m + 1, :] for m in range(micro)], axis=1)
    right = jnp.concatenate([ids.ref[2 * m + 1:2 * m + 2, :] for m in range(micro)], axis=1)
    code = jnp.where(left == 0, right, jnp.where(right == 0, left, 0)).astype(F32)
    code = jnp.broadcast_to(code, (16, tokens))
    code_out.ref[...] = jnp.zeros(code_out.ref.shape, BF16)
    code_out.ref[:, :tokens] = code.astype(BF16)
    code_out.flush()
    slot = slot_of(code[:8], tok, cap)[0:1]
    pick = (iota((slots, tokens), 0) == slot).astype(F32).astype(BF16)
    pick_out.ref[...] = pick
    pick_out.flush()
    block.ref[:slots, :] = nn(pick, grads.ref[...]).astype(BF16)
    me, _, _ = place()
    count = mine_out.ref.shape[0]
    own = count // micro
    wanted = iota((count, 1), 0)
    wanted = (wanted // own) * tok + me * own + wanted % own
    choose = (iota((count, tokens), 1) == wanted).astype(F32).astype(BF16)
    mine_out.ref[...] = nn(choose, grads.ref[...]).astype(BF16)
    mine_out.flush()
    logits = nt(router.ref[...], x.ref[...])
    apart = -jnp.sum(expert_signs(code[0:1])[0] * logits, axis=0, keepdims=True)
    parts = jnp.concatenate(split(apart) + [jnp.zeros((5, tokens), BF16)], axis=0)
    parts = jnp.concatenate(
        [nt(parts, pick), jnp.zeros((8, block.ref.shape[1] - slots), F32)], axis=1
    )
    both = jnp.concatenate([router.ref[...].astype(F32), parts], axis=0)
    block.ref[slots:, :] = both.astype(BF16)


def logit_parts(rows, slots, ways):
    apart = jnp.zeros((8, slots), F32)
    for j in range(ways):
        at = j * (slots + 16) + slots
        apart += rows[at:at + 16, :slots].astype(F32)[8:]
    return apart


def load_weights(w_ref, wbuf, sems, first):
    count = sems.shape[0]
    depth = wbuf.shape[0] // count
    copies = [
        pltpu.make_async_copy(
            w_ref.at[pl.ds(first + q * depth, depth)], wbuf.at[pl.ds(q * depth, depth)], sems.at[q]
        )
        for q in range(count)
    ]
    for copy in copies:
        copy.start()
    return copies


def load_rows(blocks, rows, sems):
    size = blocks[0].shape[0]
    loads = [
        pltpu.make_async_copy(block, rows.at[pl.ds(n * size, size)], sems.at[n])
        for n, block in enumerate(blocks)
    ]
    for load in loads:
        load.start()
    return loads


def back_kernel(ins, raws, outs, raw_outs, wbuf, sems, *, first):
    hid, back = ins[0], outs[0]
    copies = load_weights(raws[0], wbuf, sems, first)
    depth = wbuf.shape[0] // len(copies)
    hidden = hid.ref[...].T
    for q, copy in enumerate(copies):
        copy.wait()
        for part in range(4):
            rows = pl.ds(q * depth + part * (depth // 4), depth // 4)
            back.ref[rows, :] = nn(wbuf[rows, :], hidden).astype(BF16)


def mid_kernel(ins, raws, outs, raw_outs, rows, sems):
    pick, near, far, low, high = ins
    table_out, signs_out, gate_out = outs
    slots, width = pick.buffer.shape[0], near.buffer.shape[2]
    loads = load_rows(raws, rows, sems)
    me, at, odd = place()
    codes = layer_codes(near.ref, far.ref, pick.ref.shape[1])
    signs = expert_signs(nt(codes.astype(BF16), pick.ref[...]))
    layer = jnp.concatenate([jnp.full((1, 8, slots), d, jnp.int32) for d in LAYER_ORDER]) ^ me
    signs = jnp.where(layer > me, signs, 0.0)
    signs_out.ref[...] = signs
    filled = nt(jnp.ones((8, pick.buffer.shape[1]), BF16), pick.ref[...])
    for load in loads:
        load.wait()
    halves = (low.ref, high.ref)
    ways = 2 * (low.buffer.shape[0] // width)
    apart = jnp.sum(logit_parts(rows, slots, ways), axis=0, keepdims=True)
    gate = filled / (1.0 + jnp.exp(apart))
    gate_out.ref[...] = gate
    slope = gate * (1.0 - gate)
    total = jnp.zeros((slots + signs.shape[0] * 8, slots), F32)
    for way in range(0, ways, 2):
        left = jnp.concatenate([
            left_block(rows, near.ref, far.ref, block_of(at, odd, way + i), slots)
            for i in range(2)
        ], axis=1)
        at_row = way % (ways // 2) * width
        total += nn(left, halves[way * 2 // ways][at_row:at_row + 2 * width])
    base = jnp.sum(diagonal(slots) * total[:slots], axis=0, keepdims=True)
    coefs = jnp.sum(signs * total[slots:].reshape(signs.shape), axis=1)
    table = jnp.where(iota(coefs.shape, 0) == 0, base, coefs) * slope
    table = jnp.concatenate([table.astype(BF16)] * 2, axis=0)
    table_out.ref[...] = jnp.broadcast_to(table[None], table_out.ref.shape)
    table_out.flush()


def side_kernel(ins, raws, outs, raw_outs, rows, lsems, wbuf, sems, *, tok, cap):
    near, far, hid, gate = ins
    picks_out, scaled_out, codes_out, product_out, mixed_out = outs
    slots, width = hid.buffer.shape[0], near.buffer.shape[2]
    loads = load_rows(raws[:4], rows, lsems)
    copies = load_weights(raws[4], wbuf, sems, 0)
    me, at, odd = place()
    codes = layer_codes(near.ref, far.ref, codes_out.ref.shape[1])
    codes_out.ref[...] = codes
    codes_out.flush()
    slot = slot_of(codes, tok, cap)
    for i, d in enumerate(LAYER_ORDER):
        pick = (iota((slots, slot.shape[1]), 0) == slot[i:i + 1]).astype(F32).astype(BF16)
        picks_out.ref[me ^ d] = pick
    picks_out.flush()
    gate_col = jnp.sum(diagonal(slots) * gate.ref[0:1], axis=1, keepdims=True)
    scaled_out.ref[...] = (gate_col * hid.ref[...].astype(F32)).astype(BF16)
    scaled_out.flush()
    for load in loads:
        load.wait()
    ways = wbuf.shape[0] // width
    total = jnp.zeros((slots + mixed_out.ref.shape[0], mixed_out.ref.shape[1]), F32)
    for way in range(0, ways, 2):
        left = jnp.concatenate([
            left_block(rows, near.ref, far.ref, block_of(at, odd, way + i), slots)
            for i in range(2)
        ], axis=1)
        if way * len(copies) % ways == 0:
            copies[way * len(copies) // ways].wait()
        total += nn(left, wbuf[way * width:(way + 2) * width])
    product_out.ref[...] = total[:slots]
    mixed_out.ref[...] = total[slots:].astype(BF16)


def tail_kernel(ins, raws, outs, raw_outs, delta_ref, step_ref, rows, lsems, obuf, sems):
    got, picks, codes, signs, pick, scaled_in, near, far, product, mixed, gate, x, grads = ins
    blocks, down_ref = raws, raw_outs[0]
    input_out, hidden_out, router_out = outs
    layers, slots = codes.buffer.shape[0], gate.buffer.shape[1]
    tokens, width = codes.buffer.shape[1], x.buffer.shape[1]
    ways = obuf.shape[0] // width
    loads = load_rows(blocks, rows, lsems)
    for item in (product, mixed, gate, x, grads):
        item.copy.start()
    me, at, odd = place()
    parts_of = []
    for s in range(layers):
        table = got.ref[s]
        parts = nn(jnp.concatenate(split(table), axis=0), picks.ref[s])
        parts_of.append(parts[:8] + parts[8:16] + parts[16:])
    deltas = [None] * layers
    for layer in range(layers - 1, -1, -1):
        value = parts_of[layer][0:1]
        for upper in range(layer + 1, layers):
            i = LAYER_ORDER.index(layer ^ upper)
            value += deltas[upper] * parts_of[layer][i:i + 1]
        deltas[layer] = value.astype(BF16).astype(F32)
        delta_ref[layer:layer + 1, :] = deltas[layer]
    mine = jnp.concatenate([delta_ref[pl.ds(me ^ d, 1), :] for d in LAYER_ORDER], axis=0)
    delta_slot = nt(mine.astype(BF16), pick.ref[...])
    lift = (signs.ref[...] * delta_slot[:, None, :]).reshape(layers * 8, slots).astype(BF16)
    scaled = scaled_in.ref[...]
    right = jnp.concatenate([scaled, nn(lift, scaled).astype(BF16)], axis=0)
    for load in loads:
        load.wait()
    copies = []
    for way in range(ways):
        left = left_block(rows, near.ref, far.ref, block_of(at, odd, way), slots)
        obuf[way * width:(way + 1) * width] = tn(left, right).astype(BF16)
        if way % 2 == 1:
            done = pl.ds((way - 1) * width, 2 * width)
            copies.append(
                pltpu.make_async_copy(obuf.at[done], down_ref.at[done], sems.at[way // 2])
            )
            copies[-1].start()
    gate_col = jnp.sum(diagonal(slots) * gate.ref[0:1], axis=1, keepdims=True)
    hidden = product.ref[...] + tn(lift, mixed.ref[...])
    hidden_out.ref[...] = (gate_col * hidden).astype(BF16)
    hidden_out.flush()
    logit_grads = expert_signs(codes.ref[...]) * mine[:, None, :]
    router_out.ref[...] = nn(logit_grads[0].astype(BF16), x.ref[...])
    router_out.flush()
    local = jnp.concatenate([ref[17 * k] for ref in (near.ref, far.ref) for k in range(4)], axis=0)
    step_ref[...] = tn(logit_grads.reshape(layers * 8, tokens).astype(BF16), local)
    count = 4
    own, tok = grads.buffer.shape[0] // count, tokens // count
    steps = jnp.concatenate([
        step_ref[pl.ds(pl.multiple_of(m * tok + me * own, 8), own), :] for m in range(count)
    ], axis=0)
    input_out.ref[...] = (grads.ref[...].astype(F32) + steps).astype(BF16)
    input_out.flush()
    for copy in copies:
        copy.wait()


class Staged:
    def __init__(self, source, buffer, semaphore):
        self.copy = pltpu.make_async_copy(source, buffer, semaphore)
        self.buffer, self.waited = buffer, False

    @property
    def ref(self):
        if not self.waited:
            self.copy.wait()
            self.waited = True
        return self.buffer


class Result:
    def __init__(self, buffer, target, semaphore):
        self.ref, self.copy, self.sent = buffer, None, False
        self.parts = (buffer, target, semaphore)

    def flush(self):
        if not self.sent:
            self.copy = pltpu.make_async_copy(*self.parts)
            self.copy.start()
            self.sent = True


def call(kernel, staged, raw, results, raw_results=(), scratch=(), late=0, flops=0, moved=0):
    counts = (len(staged), len(raw), len(results), len(raw_results))

    def body(*refs):
        groups, at = [], 0
        for count in counts + (counts[0], counts[2]):
            groups.append(refs[at:at + count])
            at += count
        sources, raws, targets, raw_targets, ibufs, obufs = groups
        sems, rest = refs[at], refs[at + 1:]
        ins = [Staged(r, v, sems.at[n]) for n, (r, v) in enumerate(zip(sources, ibufs))]
        for item in ins[:counts[0] - late]:
            item.copy.start()
        outs = [
            Result(v, r, sems.at[counts[0] + n]) for n, (r, v) in enumerate(zip(targets, obufs))
        ]
        kernel(ins, raws, outs, raw_targets, *rest)
        for item in ins:
            item.ref
        for item in outs:
            item.flush()
        for item in outs:
            item.copy.wait()

    shapes = [jax.ShapeDtypeStruct(*o) for o in results] + [
        jax.ShapeDtypeStruct(*o) for o in raw_results
    ]
    return pl.pallas_call(
        body,
        out_shape=shapes,
        in_specs=[HBM] * (counts[0] + counts[1]),
        out_specs=[HBM] * len(shapes),
        scratch_shapes=[pltpu.VMEM(v.shape, v.dtype) for v in staged]
        + [pltpu.VMEM(*o) for o in results]
        + [pltpu.SemaphoreType.DMA((counts[0] + counts[2],))]
        + list(scratch),
        compiler_params=pltpu.CompilerParams(vmem_limit_bytes=GRANT),
        cost_estimate=pl.CostEstimate(flops=flops, bytes_accessed=moved, transcendentals=0),
    )(*staged, *raw)


def place():
    me, at = lax.axis_index("section"), lax.axis_index("dp")
    return me, at, (me & 1) == 1


def per_device(layer_inputs, expert_ids, hidden, down_weight, router_weight, grad_out):
    sections, ways = lax.axis_size("section"), lax.axis_size("dp")
    micro, tok, width = grad_out.shape
    cap, units = hidden.shape[2:]
    experts = router_weight.shape[2]
    tokens, slots = micro * tok, micro * cap
    full = ways * width
    x = layer_inputs[0].reshape(tokens, width)
    hid = hidden[0].reshape(slots, units)
    router = router_weight[0].T
    grads = grad_out.reshape(tokens, width)

    own = tok // sections
    block, pick, code, grads_mine = call(
        lambda *refs: pre_kernel(*refs, cap=cap),
        [expert_ids[0].transpose(0, 2, 1).reshape(2 * micro, tok), grads, x, router],
        [],
        [((slots + 16, width), BF16), ((slots, tokens), BF16), ((16, width), BF16),
         ((micro * own, width), BF16)],
    )

    weights = down_weight[0]

    def back(after, first):
        after, hid_after = lax.optimization_barrier((after, hid))
        return after, call(
            lambda *refs: back_kernel(*refs, first=first),
            [hid_after],
            [weights],
            [((full // 2, slots), BF16)],
            scratch=[pltpu.VMEM((full // 2, units), BF16), pltpu.SemaphoreType.DMA((2,))],
            moved=full * units,
        )[0]

    block, low = back(block, 0)
    group = [block] + [turn(block, 0, step) for step in (1, 2, 3)]
    group, low = lax.optimization_barrier((group, low))
    group = jnp.stack(group)
    routers, high = back(group[:, slots:slots + experts], full // 2)
    routers = [routers] + [turn(routers, 1, step) for step in (1, 2, 3)]
    routers, high = lax.optimization_barrier((routers, high))
    blocks = [group] + [turn(group, 1, step) for step in (1, 2, 3)]
    blocks = [b.reshape(4 * (slots + 16), width) for b in blocks]
    mine = jnp.concatenate(routers + [code[None, :experts]])
    near = jnp.concatenate([mine] + [swap(mine, "section", d) for d in SECTION_STEPS])
    far = swap(near, "section", 1)

    rows_buffer = pltpu.VMEM((ways * (slots + 16), width), BF16)
    table, signs, gate = call(
        mid_kernel,
        [pick, near, far, low, high],
        blocks,
        [
            ((sections * ways // 2, 2 * sections, slots), BF16),
            ((sections, experts, slots), F32),
            ((8, slots), F32),
        ],
        scratch=[rows_buffer, pltpu.SemaphoreType.DMA((4,))],
    )
    table = table.reshape(sections * ways, sections, slots)
    got_table = lax.all_to_all(table, ("section", "dp"), 0, 0, tiled=True)

    table_sum = jnp.sum(
        got_table.reshape(sections, ways, sections, slots).astype(F32), axis=1
    )
    picks, scaled, codes, product, mixed = call(
        lambda *refs: side_kernel(*refs, tok=tok, cap=cap),
        [near, far, hid, gate],
        blocks + [weights],
        [
            ((sections, slots, tokens), BF16),
            ((slots, units), BF16),
            ((sections, tokens), F32),
            ((slots, units), F32),
            ((sections * experts, units), BF16),
        ],
        scratch=[
            rows_buffer,
            pltpu.SemaphoreType.DMA((4,)),
            pltpu.VMEM((full, units), BF16),
            pltpu.SemaphoreType.DMA((4,)),
        ],
        flops=10**9,
        moved=10**7,
    )
    input_grad, hidden_grad, router_grad, down_grad = call(
        tail_kernel,
        [
            table_sum, picks, codes, signs, pick, scaled, near, far,
            product, mixed, gate, x, grads_mine,
        ],
        blocks,
        [
            ((micro * own, width), BF16),
            ((slots, units), BF16),
            ((experts, width), F32),
        ],
        raw_results=[((full, units), BF16)],
        scratch=[
            pltpu.VMEM((sections, tokens), F32),
            pltpu.VMEM((tokens, width), F32),
            rows_buffer,
            pltpu.SemaphoreType.DMA((4,)),
            pltpu.VMEM((full, units), BF16),
            pltpu.SemaphoreType.DMA((ways // 2,)),
        ],
        late=5,
        flops=2 * 192 * full * units,
        moved=full * units * 2,
    )
    return (
        input_grad.reshape(micro, own, width),
        hidden_grad.reshape(1, micro, cap, units),
        down_grad[None],
        router_grad.T[None],
    )


def solution(mesh):
    return jax.shard_map(
        per_device,
        mesh=mesh,
        in_specs=(
            P("section", None, None, "dp"),
            P("section", None, None, None),
            P("section", None, None, "dp"),
            P("section", None, "dp"),
            P("section", "dp", None),
            P(None, None, "dp"),
        ),
        out_specs=(
            P(None, "section", "dp"),
            P("section", None, None, "dp"),
            P("section", None, "dp"),
            P("section", "dp", None),
        ),
        check_vma=False,
    )
```
